32 devices in a mesh: dp: 8 (over z, x), tensor: 4 (over y, core).
Axes of the slice: x: 2, y: 2, z: 4, core: 2. Of those that a mesh axis runs over, the one named last changes fastest.
Arguments:
- tokens: bfloat16 [16384, 768], P(('dp', 'tensor')), may hold values from -6 to 6
- segment_ids: int32 [16384], P('dp'), may hold values from -1 to 7, as said below
- ln1_gain: float32 [768], replicated, may hold values from 0.5 to 1.5
- ln1_bias: float32 [768], replicated, may hold values from -1.25 to 1.25
- ln2_gain: float32 [768], replicated, may hold values from 0.5 to 1.5
- ln2_bias: float32 [768], replicated, may hold values from -1.25 to 1.25
- w_qkv: bfloat16 [768, 2304], P('dp', 'tensor'), may hold values from -0.21875 to 0.21875
- b_qkv: float32 [2304], P('tensor'), may hold values from -1.25 to 1.25
- w_dense: bfloat16 [768, 768], P('dp', 'tensor'), may hold values from -2.5 to 2.5
- b_dense: float32 [768], replicated, may hold values from -1.25 to 1.25
- w_fc1: bfloat16 [768, 3072], P('dp', 'tensor'), may hold values from -0.21875 to 0.21875
- b_fc1: float32 [3072], P('tensor'), may hold values from -1.25 to 1.25
- w_fc2: bfloat16 [768, 3072], P('dp', 'tensor'), may hold values from -0.109375 to 0.109375
- b_fc2: float32 [768], replicated, may hold values from -1.25 to 1.25
- cotangent: bfloat16 [16384, 768], P(('dp', 'tensor')), may hold values from -6 to 6
Outputs:
- out: bfloat16 [16384, 768], P(('dp', 'tensor'))
- input_grad: float32 [16384, 768], P(('dp', 'tensor'))
- ln1_gain_grad: float32 [768], P(('dp', 'tensor'))
- ln1_bias_grad: float32 [768], P(('dp', 'tensor'))
- ln2_gain_grad: float32 [768], P(('dp', 'tensor'))
- ln2_bias_grad: float32 [768], P(('dp', 'tensor'))
- w_qkv_grad: float32 [768, 2304], P('dp', 'tensor')
- b_qkv_grad: float32 [2304], P(('tensor', 'dp'))
- w_dense_grad: float32 [768, 768], P('dp', 'tensor')
- b_dense_grad: float32 [768], P(('dp', 'tensor'))
- w_fc1_grad: float32 [768, 3072], P('dp', 'tensor')
- b_fc1_grad: float32 [3072], P(('tensor', 'dp'))
- w_fc2_grad: float32 [768, 3072], P('dp', 'tensor')
- b_fc2_grad: float32 [768], P(('dp', 'tensor'))
The draws below stay inside these ranges and needn't reach their ends.
Inputs may be any that keep to these rules, and one draw needn't show every extreme that they name: `segment_ids`: each group of 2048 rows (one index of dp) holds one whole sequence from its first row, of more than 1536 rows, and padding rows with id -1 after it; the sequences' ids are distinct; in every draw some group's sequence fills all 2048 rows.
All inputs are finite; a program needn't handle non-finite values.
Results may differ from the reference program's by a relative error of at most 0.013.
Values may be sent and summed in bfloat16 or wider, within the bound.
No kernel may reach another device: no remote copies, remote signals or barrier semaphores. Data moves between devices by JAX's collectives and lax.ppermute only.
A program may use at most 128 MiB of HBM per device.

```python
import jax
import jax.numpy as jnp
from jax import lax

HEADS = 12
HEAD = 64
ROT = 16
FF = 3072
TOK_DEV = 512
D = 768
GROUP = 2048
TOKENS = 16384
N_DP = 8


def draw_segment_ids(key, part):
    key = jax.random.fold_in(key, 11)
    first_key, second_key, third_key = jax.random.split(key, 3)
    surplus = jax.random.randint(first_key, (N_DP,), 0, TOK_DEV)
    full_group = jax.random.randint(second_key, (), 0, N_DP)
    lengths = GROUP - TOK_DEV + 1 + surplus
    lengths = jnp.where(jnp.arange(N_DP, dtype=jnp.int32) == full_group, GROUP, lengths)
    numbers = jax.random.permutation(third_key, N_DP).astype(jnp.int32)
    row_index = jnp.arange(GROUP, dtype=jnp.int32)
    labels = jnp.where(row_index[None, :] < lengths[:, None], numbers[:, None], -1)
    return labels.reshape(N_DP * GROUP).astype(jnp.int32)


def strengthened(values, own_key, source, target, blocks, factor):
    def block_of(dim):
        return (jnp.arange(values.shape[dim]) // (values.shape[dim] // blocks)).reshape((-1,) + (1,) * (values.ndim - 1 - dim))

    first = jax.random.permutation(own_key, blocks)[block_of(target)]
    far = (block_of(target) + blocks // 2) % blocks
    return jnp.where((block_of(source) == first) | (block_of(source) == far), factor * values, values)


def level_of(own_key, extent, cuts, least, largest):
    factor_of = 1.0
    for dim, blocks in cuts:
        steps = jax.random.uniform(jax.random.fold_in(jax.random.fold_in(own_key, 6), dim), (blocks,), jnp.float32, least / len(cuts), largest / len(cuts))
        factor_of = factor_of * jnp.repeat(jnp.exp(steps), extent[dim] // blocks).reshape((-1,) + (1,) * (len(extent) - 1 - dim))
    return factor_of


def normal_values(key, shape, scale, reach, cuts=(), kind=jnp.bfloat16):
    array = jax.random.normal(key, shape, jnp.float32) * scale
    if len(cuts) > 0:
        array = level_of(key, shape, cuts, -0.22, 0.18) * array
    return jnp.clip(array, min=-reach, max=reach).astype(kind)


def heavy_noise(stream_key, extent, deviation, limit, cuts, heavy, held_as=jnp.bfloat16):
    values = deviation * jax.random.normal(stream_key, extent, jnp.float32)
    if cuts:
        values = values * level_of(stream_key, extent, cuts, -0.22, 0.18)
    return jnp.clip(strengthened(values, jax.random.fold_in(stream_key, 3), *heavy), -limit, limit).astype(held_as)


def setup_inputs(seed: int = 0) -> dict:
    seeds = jax.random.split(jax.random.key(seed), 16)
    tokens = normal_values(seeds[0], (TOKENS, D), 1.0, 6.0, ((0, 32),))
    segment_ids = draw_segment_ids(jax.random.fold_in(seeds[15], 71), 0)
    ln1_gain = jnp.clip(1.0 + 0.1 * jax.random.normal(seeds[2], (D,), jnp.float32), 0.5, 1.5)
    ln1_bias = normal_values(seeds[3], (D,), 0.2, 1.25, (), jnp.float32)
    ln2_gain = jnp.clip(1.0 + 0.1 * jax.random.normal(seeds[4], (D,), jnp.float32), 0.5, 1.5)
    ln2_bias = normal_values(seeds[5], (D,), 0.2, 1.25, (), jnp.float32)
    w_qkv = normal_values(seeds[6], (D, 3 * D), D ** -0.5, 0.21875, ((0, 8), (1, 4)))
    b_qkv = normal_values(seeds[7], (3 * D,), 0.2, 1.25, ((0, 4),), jnp.float32)
    w_dense = normal_values(seeds[8], (D, D), (max(1, 16 * D // GROUP)) ** -0.5, 2.5, ((0, 8), (1, 4)))
    b_dense = normal_values(seeds[9], (D,), 0.2, 1.25, (), jnp.float32)
    w_fc1 = normal_values(seeds[10], (D, FF), D ** -0.5, 0.21875, ((0, 8), (1, 4)))
    b_fc1 = normal_values(seeds[11], (FF,), 0.2, 1.25, ((0, 4),), jnp.float32)
    w_fc2 = normal_values(seeds[12], (D, FF), FF ** -0.5, 0.109375, ((0, 8), (1, 4)))
    b_fc2 = normal_values(seeds[13], (D,), 0.2, 1.25, (), jnp.float32)
    cotangent = heavy_noise(seeds[14], (TOKENS, D), 1.0, 6.0, ((0, 32),), (0, 1, 32, 2.75))
    return {"tokens": tokens, "segment_ids": segment_ids, "ln1_gain": ln1_gain, "ln1_bias": ln1_bias, "ln2_gain": ln2_gain, "ln2_bias": ln2_bias, "w_qkv": w_qkv, "b_qkv": b_qkv, "w_dense": w_dense, "b_dense": b_dense, "w_fc1": w_fc1, "b_fc1": b_fc1, "w_fc2": w_fc2, "b_fc2": b_fc2, "cotangent": cotangent}


EPS = 1e-05
NEG = -1e+30
HIGH = lax.Precision.HIGHEST

@jax.custom_vjp
def low(v):
    return lax.optimization_barrier(v.astype(jnp.bfloat16)).astype(jnp.float32)

@jax.custom_vjp
def low_back(v):
    return v

def low_keep(v):
    return (low(v), None)

def low_pass(kept, grad):
    return (grad,)

def back_keep(v):
    return (v, None)

def back_low(kept, grad):
    return (low(grad),)
low.defvjp(low_keep, low_pass)
low_back.defvjp(back_keep, back_low)

def layer_norm(values, gain, bias):
    center = values - lax.optimization_barrier(jnp.mean(values, axis=-1, keepdims=True))
    spread = lax.optimization_barrier(jnp.mean(center * center, axis=-1, keepdims=True))
    return center * lax.rsqrt(spread + EPS) * gain + bias

def angle_tables(seg_rows):
    count = seg_rows.shape[0]
    row_index = jnp.arange(count, dtype=jnp.int32)
    prior = jnp.concatenate([seg_rows[:1] - 1, seg_rows[:-1]])
    starts = lax.cummax(jnp.where(seg_rows != prior, row_index, 0), axis=0)
    places = (row_index - starts).astype(jnp.float32)
    inverse = 10000.0 ** (-jnp.arange(0, ROT, 2, dtype=jnp.float32) / ROT)
    angles = places[:, None] * inverse[None, :]
    angles = jnp.concatenate([angles, angles], axis=-1)
    return (jnp.cos(angles)[:, None, :], jnp.sin(angles)[:, None, :])

def rotate(parts, cosine, sine):
    half = ROT // 2
    front = parts[..., :ROT]
    turned = jnp.concatenate([-front[..., half:], front[..., :half]], axis=-1)
    return jnp.concatenate([front * cosine + turned * sine, parts[..., ROT:]], axis=-1)

def attention(queries, keys, values, seg_rows):
    count = keys.shape[0]
    block_rows = min(512, count)
    key_index = jnp.arange(count, dtype=jnp.int32)
    scale = HEAD ** (-0.5)

    def one_block(begin):
        query_block = lax.dynamic_slice_in_dim(queries, begin, block_rows, 0)
        query_segs = lax.dynamic_slice_in_dim(seg_rows, begin, block_rows, 0)
        raw = jnp.einsum('qhd,khd->hqk', query_block, keys, precision=HIGH)
        query_index = begin + jnp.arange(block_rows, dtype=jnp.int32)
        allowed = (query_segs[:, None] == seg_rows[None, :]) & (key_index[None, :] <= query_index[:, None])
        scores = low_back(jnp.where(allowed[None], raw * scale, NEG))
        top = lax.optimization_barrier(jnp.max(scores, axis=-1, keepdims=True))
        expo = jnp.exp(scores - top)
        probs = low(expo / lax.optimization_barrier(jnp.sum(expo, axis=-1, keepdims=True)))
        return jnp.einsum('hqk,khd->qhd', probs, values, precision=HIGH)
    begins = jnp.arange(count // block_rows, dtype=jnp.int32) * block_rows
    return lax.map(jax.checkpoint(one_block), begins).reshape(count, HEADS, HEAD)

def group_forward(params, rows_in, seg_rows):
    gain_one, bias_one, gain_two, bias_two, qkv_w, qkv_b, dense_w, dense_b, up_w, up_b, down_w, down_b = params
    count = rows_in.shape[0]
    cosine, sine = angle_tables(seg_rows)
    normed_one = low(layer_norm(rows_in, gain_one, bias_one))
    normed_two = low(layer_norm(rows_in, gain_two, bias_two))
    mixed = low_back(jnp.dot(normed_one, qkv_w, precision=HIGH) + qkv_b).reshape(count, HEADS, 3 * HEAD)
    queries = low(rotate(mixed[..., :HEAD], cosine, sine))
    keys = low(rotate(mixed[..., HEAD:2 * HEAD], cosine, sine))
    values = low(mixed[..., 2 * HEAD:])
    attended = low_back(low(attention(queries, keys, values, seg_rows))).reshape(count, D)
    hidden = low_back(jnp.dot(normed_two, up_w, precision=HIGH) + up_b)
    active = low(jax.nn.gelu(hidden, approximate=False))
    branch = jnp.dot(attended, dense_w.T, precision=HIGH) + jnp.dot(active, down_w.T, precision=HIGH)
    return rows_in + branch + dense_b + down_b

def reference(tokens, segment_ids, ln1_gain, ln1_bias, ln2_gain, ln2_bias, w_qkv, b_qkv, w_dense, b_dense, w_fc1, b_fc1, w_fc2, b_fc2, cotangent):
    params = tuple((item.astype(jnp.float32) for item in (ln1_gain, ln1_bias, ln2_gain, ln2_bias, w_qkv, b_qkv, w_dense, b_dense, w_fc1, b_fc1, w_fc2, b_fc2)))
    inputs = tokens.astype(jnp.float32).reshape(N_DP, GROUP, D)
    grads_out = cotangent.astype(jnp.float32).reshape(N_DP, GROUP, D)
    segments = segment_ids.astype(jnp.int32).reshape(N_DP, GROUP)

    def group_step(totals, pieces):
        rows_in, rows_grad, seg_rows = pieces
        result, pull = jax.vjp(lambda weights, values: group_forward(weights, values, seg_rows), params, rows_in)
        param_grads, input_part = pull(rows_grad)
        totals = jax.tree.map(lambda left, right: left + right, totals, param_grads)
        return (totals, (result.astype(jnp.bfloat16), input_part))
    zeros = tuple((jnp.zeros_like(item) for item in params))
    totals, (results, input_parts) = lax.scan(group_step, zeros, (inputs, grads_out, segments))
    return (results.reshape(TOKENS, D), input_parts.reshape(TOKENS, D)) + totals
```

```python
import functools

import jax
import jax.numpy as jnp
from jax import lax
from jax.experimental import pallas as pl
from jax.experimental.pallas import tpu as pltpu
from jax.sharding import PartitionSpec as P

HEAD = 64
ROT = 16
HALF = ROT // 2
EPS = 1e-05
NEG = -1e30
SCALE = HEAD ** (-0.5)
WHOLE = 1536
BLOCK = 512
F32 = jnp.float32
BF16 = jnp.bfloat16
VMEM_LIMIT = 56 * 1024 * 1024


def dot(left, right):
    return jnp.dot(left, right, preferred_element_type=F32)


def dot_nt(left, right):
    return lax.dot_general(left, right, (((1,), (1,)), ((), ())), preferred_element_type=F32)


def call(kernel, grid, in_specs, out_specs, out_shape, scratch, name, prefetch=0):
    return pl.pallas_call(
        kernel,
        grid_spec=pltpu.PrefetchScalarGridSpec(
            num_scalar_prefetch=prefetch,
            grid=grid,
            in_specs=in_specs,
            out_specs=out_specs,
            scratch_shapes=scratch,
        ),
        out_shape=out_shape,
        compiler_params=pltpu.CompilerParams(vmem_limit_bytes=VMEM_LIMIT),
        name=name,
    )


def whole_spec(shape):
    return pl.BlockSpec(shape, lambda *_: (0,) * len(shape))


def standardize(block):
    values = block.astype(F32)
    center = values - jnp.mean(values, axis=0, keepdims=True)
    spread = jnp.mean(center * center, axis=0, keepdims=True)
    return center * lax.rsqrt(spread + EPS)


def project_kernel(place, x_ref, w_ref, b_ref, gain_ref, bias_ref, cos_ref, sin_ref, out_ref, wt):
    @pl.when(pl.program_id(0) == 0)
    def _():
        wt[...] = w_ref[...].T

    normed = (standardize(x_ref[0]) * gain_ref[...] + bias_ref[...]).astype(BF16)
    cosine, sine = cos_ref[...], sin_ref[...]
    for head in range(w_ref.shape[1] // (3 * HEAD)):
        base = head * 3 * HEAD
        mixed = dot(wt[base : base + 3 * HEAD, :], normed) + b_ref[base : base + 3 * HEAD, :]
        for part, factor in ((0, SCALE), (HEAD, 1.0)):
            one, two = mixed[part : part + HALF], mixed[part + HALF : part + ROT]
            turned = jnp.concatenate(
                [one * cosine - two * sine, two * cosine + one * sine, mixed[part + ROT : part + HEAD]],
                axis=0,
            )
            out_ref[base + part : base + part + HEAD, :] = (turned * factor).astype(BF16)
        out_ref[base + 2 * HEAD : base + 3 * HEAD, :] = mixed[2 * HEAD :].astype(BF16)


def project(place, x_all, w, b, gain, bias, cosine, sine):
    parts, width, slab = x_all.shape
    cols = w.shape[1]
    return call(
        project_kernel,
        (parts,),
        [
            pl.BlockSpec((1, width, slab), lambda s, t: (s ^ t[0], 0, 0)),
            whole_spec(w.shape),
            whole_spec(b.shape),
            whole_spec(gain.shape),
            whole_spec(bias.shape),
            pl.BlockSpec((HALF, slab), lambda s, t: (0, s)),
            pl.BlockSpec((HALF, slab), lambda s, t: (0, s)),
        ],
        pl.BlockSpec((cols, slab), lambda s, t: (0, s)),
        jax.ShapeDtypeStruct((cols, parts * slab), BF16),
        [pltpu.VMEM((cols, width), BF16)],
        "project",
        prefetch=1,
    )(place, x_all, w, b, gain, bias, cosine, sine)


def masked(scores, first_key, first_query, starts):
    diagonal = first_key + scores.shape[0] > first_query
    ragged = first_query + scores.shape[1] > WHOLE
    if not (diagonal or ragged):
        return scores
    key = first_key + lax.broadcasted_iota(jnp.int32, scores.shape, 0)
    allowed = key >= starts
    if diagonal:
        allowed &= key <= first_query + lax.broadcasted_iota(jnp.int32, scores.shape, 1)
    return jnp.where(allowed, scores, NEG)


def attend_kernel(start_ref, qkv_ref, out_ref, lse_ref, keys, held):
    rows = qkv_ref.shape[1]
    block = min(BLOCK, rows)
    keys[...] = qkv_ref[HEAD : 2 * HEAD, :].T
    for begin in range(0, rows, block):
        here = slice(begin, begin + block)
        queries, starts = qkv_ref[0:HEAD, here], start_ref[0:1, here]
        top = jnp.full((1, block), NEG, F32)
        for first in range(0, begin + block, block):
            scores = masked(dot(keys[first : first + block, :], queries), first, begin, starts)
            held[first : first + block, :] = scores
            top = jnp.maximum(top, jnp.max(scores, axis=0, keepdims=True))
        total = jnp.zeros((1, block), F32)
        result = jnp.zeros((HEAD, block), F32)
        for first in range(0, begin + block, block):
            expo = jnp.exp(held[first : first + block, :] - top)
            total += jnp.sum(expo, axis=0, keepdims=True)
            result += dot(qkv_ref[2 * HEAD : 3 * HEAD, first : first + block], expo.astype(BF16))
        out_ref[:, here] = (result / total).astype(BF16)
        lse_ref[0, 0:1, here] = top + jnp.log(total)


def attend(starts, qkv):
    rows = qkv.shape[1]
    heads = qkv.shape[0] // (3 * HEAD)
    return call(
        attend_kernel,
        (heads,),
        [whole_spec(starts.shape), pl.BlockSpec((3 * HEAD, rows), lambda h: (h, 0))],
        [pl.BlockSpec((HEAD, rows), lambda h: (h, 0)), pl.BlockSpec((1, 1, rows), lambda h: (h, 0, 0))],
        [jax.ShapeDtypeStruct((heads * HEAD, rows), BF16), jax.ShapeDtypeStruct((heads, 1, rows), F32)],
        [pltpu.VMEM((rows, HEAD), BF16), pltpu.VMEM((rows, min(BLOCK, rows)), F32)],
        "attend",
    )(starts, qkv)


def attend_back_kernel(
    start_ref, cos_ref, sin_ref, qkv_ref, grad_ref, out_ref, lse_ref, mixed_ref, keys, values, key_sum, value_sum
):
    rows = qkv_ref.shape[1]
    block = min(BLOCK, rows)
    keys[...] = qkv_ref[HEAD : 2 * HEAD, :].T
    values[...] = qkv_ref[2 * HEAD : 3 * HEAD, :].T
    key_sum[...] = jnp.zeros_like(key_sum)
    value_sum[...] = jnp.zeros_like(value_sum)

    def put_unrotated(base, here, grads):
        cosine, sine = cos_ref[:, here], sin_ref[:, here]
        one, two = grads[0:HALF, :], grads[HALF:ROT, :]
        turned = jnp.concatenate(
            [one * cosine + two * sine, two * cosine - one * sine, grads[ROT:, :]], axis=0
        )
        mixed_ref[base : base + HEAD, here] = turned.astype(BF16)

    for begin in range(0, rows, block):
        here = slice(begin, begin + block)
        queries, grads, starts = qkv_ref[0:HEAD, here], grad_ref[:, here], start_ref[0:1, here]
        lse = lse_ref[0, 0:1, here]
        inner = jnp.sum(grads.astype(F32) * out_ref[:, here].astype(F32), axis=0, keepdims=True)
        query_rows, grad_rows = queries.T, grads.T
        query_sum = jnp.zeros((HEAD, block), F32)
        for first in range(0, begin + block, block):
            there = slice(first, first + block)
            scores = masked(dot(keys[there, :], queries), first, begin, starts)
            probs = jnp.exp(scores - lse)
            score_grads = (probs * (dot(values[there, :], grads) - inner)).astype(BF16)
            query_sum += dot(qkv_ref[HEAD : 2 * HEAD, there], score_grads)
            key_sum[there, :] += dot(score_grads, query_rows)
            value_sum[there, :] += dot(probs.astype(BF16), grad_rows)
        put_unrotated(0, here, query_sum * SCALE)
    put_unrotated(HEAD, slice(0, rows), key_sum[...].T)
    mixed_ref[2 * HEAD : 3 * HEAD, :] = value_sum[...].T.astype(BF16)


def attend_back(starts, cosine, sine, qkv, grads, out, lse):
    rows = qkv.shape[1]
    heads = qkv.shape[0] // (3 * HEAD)
    head_block = pl.BlockSpec((HEAD, rows), lambda h: (h, 0))
    three_block = pl.BlockSpec((3 * HEAD, rows), lambda h: (h, 0))
    return call(
        attend_back_kernel,
        (heads,),
        [
            whole_spec(starts.shape),
            whole_spec(cosine.shape),
            whole_spec(sine.shape),
            three_block,
            head_block,
            head_block,
            pl.BlockSpec((1, 1, rows), lambda h: (h, 0, 0)),
        ],
        three_block,
        jax.ShapeDtypeStruct((heads * 3 * HEAD, rows), BF16),
        [pltpu.VMEM((rows, HEAD), BF16)] * 2 + [pltpu.VMEM((rows, HEAD), F32)] * 2,
        "attend_back",
    )(starts, cosine, sine, qkv, grads, out, lse)


def feed_kernel(
    place,
    x_ref,
    dy_ref,
    att_ref,
    up_ref,
    down_ref,
    dense_ref,
    b_ref,
    gain_ref,
    bias_ref,
    branch_ref,
    normed_ref,
    att_grad_ref,
    weights_ref,
    vector_ref,
    up_t,
    down_t,
    dense_t,
    active,
    hidden_grad,
    sums,
    vectors,
):
    step = pl.program_id(0)
    width, hidden_count = up_ref.shape
    dense_count = dense_ref.shape[1]

    @pl.when(step == 0)
    def _():
        up_t[...] = up_ref[...].T
        down_t[...] = down_ref[...].T
        dense_t[...] = dense_ref[...].T
        sums[...] = jnp.zeros_like(sums)
        vectors[...] = jnp.zeros_like(vectors)

    unit = standardize(x_ref[0])
    normed = (unit * gain_ref[...] + bias_ref[...]).astype(BF16)
    dy = dy_ref[0]
    attended = att_ref[...]
    att_grad_ref[...] = dot(dense_t[...], dy).astype(BF16)
    chunk = min(256, hidden_count)
    for first in range(0, hidden_count, chunk):
        units = slice(first, first + chunk)
        hidden = dot(up_t[units, :], normed) + b_ref[units, :]
        chance = 0.5 + 0.5 * lax.erf(hidden * (0.5**0.5))
        density = jnp.exp(hidden * hidden * -0.5) * (hidden * 0.3989422804014327)
        now = (hidden * chance).astype(BF16)
        back = (dot(down_t[units, :], dy) * (chance + density)).astype(BF16)
        active[units, :] = now
        hidden_grad[units, :] = back
        sums[:, units] += dot_nt(normed, back)
        sums[:, hidden_count + first : hidden_count + first + chunk] += dot_nt(dy, now)
        vectors[units, 3:4] += jnp.sum(back.astype(F32), axis=1, keepdims=True)
    sums[:, 2 * hidden_count :] += dot_nt(dy, attended)
    branch_ref[0] = (dot(dense_ref[...], attended) + dot(down_ref[...], active[...])).astype(BF16)
    normed_grad = dot(up_ref[...], hidden_grad[...])
    normed_ref[0] = normed_grad * gain_ref[...]
    vectors[:, 0:1] += jnp.sum(normed_grad * unit, axis=1, keepdims=True)
    vectors[:, 1:2] += jnp.sum(normed_grad, axis=1, keepdims=True)
    vectors[:, 2:3] += jnp.sum(dy.astype(F32), axis=1, keepdims=True)

    @pl.when(step == pl.num_programs(0) - 1)
    def _():
        weights_ref[...] = sums[...].astype(BF16)
        vector_ref[...] = vectors[...]


def feed(place, x_all, dy_all, attended, up, down, dense, b, gain, bias):
    parts, width, slab = x_all.shape
    hidden_count, dense_count = up.shape[1], dense.shape[1]
    grad_cols = 2 * hidden_count + dense_count
    slab_block = pl.BlockSpec((1, width, slab), lambda s, t: (s ^ t[0], 0, 0))
    out_block = pl.BlockSpec((1, width, slab), lambda s, t: (s, 0, 0))
    rows_block = pl.BlockSpec((dense_count, slab), lambda s, t: (0, s))
    return call(
        feed_kernel,
        (parts,),
        [
            slab_block,
            slab_block,
            rows_block,
            whole_spec(up.shape),
            whole_spec(down.shape),
            whole_spec(dense.shape),
            whole_spec(b.shape),
            whole_spec(gain.shape),
            whole_spec(bias.shape),
        ],
        [out_block, out_block, rows_block, whole_spec((width, grad_cols)), whole_spec((hidden_count, 4))],
        [
            jax.ShapeDtypeStruct((parts, width, slab), BF16),
            jax.ShapeDtypeStruct((parts, width, slab), F32),
            jax.ShapeDtypeStruct((dense_count, parts * slab), BF16),
            jax.ShapeDtypeStruct((width, grad_cols), BF16),
            jax.ShapeDtypeStruct((hidden_count, 4), F32),
        ],
        [
            pltpu.VMEM((hidden_count, width), BF16),
            pltpu.VMEM((hidden_count, width), BF16),
            pltpu.VMEM((dense_count, width), BF16),
            pltpu.VMEM((hidden_count, slab), BF16),
            pltpu.VMEM((hidden_count, slab), BF16),
            pltpu.VMEM((width, grad_cols), F32),
            pltpu.VMEM((hidden_count, 4), F32),
        ],
        "feed",
        prefetch=1,
    )(place, x_all, dy_all, attended, up, down, dense, b, gain, bias)


def project_back_kernel(
    place, x_ref, mixed_ref, part_ref, w_ref, gain_ref, bias_ref, unit_ref, weights_ref, vector_ref, count_ref, sums, vectors, counts
):
    step = pl.program_id(0)

    @pl.when(step == 0)
    def _():
        sums[...] = jnp.zeros_like(sums)
        vectors[...] = jnp.zeros_like(vectors)
        counts[...] = jnp.zeros_like(counts)

    unit = standardize(x_ref[0])
    normed = (unit * gain_ref[...] + bias_ref[...]).astype(BF16)
    mixed = mixed_ref[...]
    sums[...] += dot_nt(normed, mixed)
    counts[...] += jnp.sum(mixed.astype(F32), axis=1, keepdims=True)
    normed_grad = dot(w_ref[...], mixed)
    unit_ref[0] = (part_ref[0] + normed_grad * gain_ref[...]).astype(BF16)
    vectors[:, 0:1] += jnp.sum(normed_grad * unit, axis=1, keepdims=True)
    vectors[:, 1:2] += jnp.sum(normed_grad, axis=1, keepdims=True)

    @pl.when(step == pl.num_programs(0) - 1)
    def _():
        weights_ref[...] = sums[...].astype(BF16)
        vector_ref[...] = vectors[...]
        count_ref[...] = counts[...]


def project_back(place, x_all, mixed, part, w, gain, bias):
    parts, width, slab = x_all.shape
    cols = w.shape[1]
    slab_block = pl.BlockSpec((1, width, slab), lambda s, t: (s ^ t[0], 0, 0))
    out_block = pl.BlockSpec((1, width, slab), lambda s, t: (s, 0, 0))
    return call(
        project_back_kernel,
        (parts,),
        [
            slab_block,
            pl.BlockSpec((cols, slab), lambda s, t: (0, s)),
            out_block,
            whole_spec(w.shape),
            whole_spec(gain.shape),
            whole_spec(bias.shape),
        ],
        [out_block, whole_spec((width, cols)), whole_spec((width, 2)), whole_spec((cols, 1))],
        [
            jax.ShapeDtypeStruct((parts, width, slab), BF16),
            jax.ShapeDtypeStruct((width, cols), BF16),
            jax.ShapeDtypeStruct((width, 2), F32),
            jax.ShapeDtypeStruct((cols, 1), F32),
        ],
        [pltpu.VMEM((width, cols), F32), pltpu.VMEM((width, 2), F32), pltpu.VMEM((cols, 1), F32)],
        "project_back",
        prefetch=1,
    )(place, x_all, mixed, part, w, gain, bias)


def swap(value, bit):
    count = lax.axis_size("tensor")
    return lax.ppermute(value, "tensor", [(i, i ^ bit) for i in range(count)])


def gather_group(own):
    far = swap(own, 2)
    near = swap(own, 1)
    return jnp.stack([own, near, far, swap(far, 1)])


def scatter_group(slabs, mine):
    def pick(r):
        return lax.dynamic_index_in_dim(slabs, mine ^ r, 0, keepdims=False)

    far = pick(2).astype(F32) + swap(pick(3), 1).astype(F32)
    near = pick(0).astype(F32) + swap(pick(1), 1).astype(F32)
    return near + swap(far.astype(BF16), 2).astype(F32)


def body(
    tokens,
    segment_ids,
    ln1_gain,
    ln1_bias,
    ln2_gain,
    ln2_bias,
    w_qkv,
    b_qkv,
    w_dense,
    b_dense,
    w_fc1,
    b_fc1,
    w_fc2,
    b_fc2,
    cotangent,
):
    group_rows = segment_ids.shape[0]
    width = tokens.shape[1]
    own_width = w_qkv.shape[0]
    mine = lax.axis_index("tensor").astype(jnp.int32)
    place = mine.reshape(1)

    x_all = gather_group(tokens.T)
    qkv_full = lax.all_gather(w_qkv, "dp", axis=0, tiled=True)
    dense_full = lax.all_gather(w_dense, "dp", axis=0, tiled=True)
    dy_all = gather_group(cotangent.T)
    up_full = lax.all_gather(w_fc1, "dp", axis=0, tiled=True)
    down_full = lax.all_gather(w_fc2, "dp", axis=0, tiled=True)

    row = jnp.arange(group_rows, dtype=jnp.int32)
    padding = segment_ids != segment_ids[0]
    length = jnp.sum(jnp.where(padding, 0, 1))
    starts = jnp.where(padding, length, 0)
    inverse = 10000.0 ** (-jnp.arange(0, ROT, 2, dtype=F32) / ROT)
    angles = inverse[:, None] * (row - starts).astype(F32)[None, :]
    cosine, sine = jnp.cos(angles), jnp.sin(angles)
    starts = starts[None, :]

    gain_one, bias_one = ln1_gain[:, None], ln1_bias[:, None]
    gain_two, bias_two = ln2_gain[:, None], ln2_bias[:, None]
    qkv = project(place, x_all, qkv_full, b_qkv[:, None], gain_one, bias_one, cosine, sine)
    attended, lse = attend(starts, qkv)
    branch, part, att_grad, feed_grads, feed_vectors = feed(
        place, x_all, dy_all, attended, up_full, down_full, dense_full, b_fc1[:, None], gain_two, bias_two
    )
    extra = jnp.pad(feed_vectors.astype(BF16), ((0, 0), (0, 124)))
    feed_owned = lax.psum_scatter(
        jnp.concatenate([feed_grads, extra], axis=1), "dp", scatter_dimension=0, tiled=True
    ).astype(F32)
    summed = scatter_group(branch, mine)
    own_input = tokens.astype(F32)
    out = (own_input + summed.T + b_dense + b_fc2).astype(BF16)

    mixed_grad = attend_back(starts, cosine, sine, qkv, att_grad, attended, lse)
    unit_grad, qkv_grad, qkv_vectors, qkv_bias_grad = project_back(
        place, x_all, mixed_grad, part, qkv_full, gain_one, bias_one
    )
    bias_own = qkv_bias_grad.shape[0] // lax.axis_size("dp")
    bias_rows = jnp.pad(qkv_bias_grad.reshape(-1, bias_own), ((0, 0), (0, own_width - bias_own)))
    extra = jnp.concatenate([qkv_vectors, bias_rows.reshape(width, 1)], axis=1)
    extra = jnp.pad(extra.astype(BF16), ((0, 0), (0, 125)))
    qkv_owned = lax.psum_scatter(
        jnp.concatenate([qkv_grad, extra], axis=1), "dp", scatter_dimension=0, tiled=True
    ).astype(F32)
    unit_sum = scatter_group(unit_grad, mine).T

    center = own_input - jnp.mean(own_input, axis=-1, keepdims=True)
    inverse_scale = lax.rsqrt(jnp.mean(center * center, axis=-1, keepdims=True) + EPS)
    unit = center * inverse_scale
    input_grad = cotangent.astype(F32) + inverse_scale * (
        unit_sum
        - jnp.mean(unit_sum, axis=-1, keepdims=True)
        - unit * jnp.mean(unit_sum * unit, axis=-1, keepdims=True)
    )

    cols = w_qkv.shape[1]
    hidden_count = w_fc1.shape[1]
    dense_count = w_dense.shape[1]
    up_end, down_end = hidden_count, 2 * hidden_count
    dense_end = down_end + dense_count
    norms = jnp.concatenate(
        [qkv_owned[:, cols : cols + 2], feed_owned[:, dense_end : dense_end + 2]], axis=1
    )
    norms = norms.T.reshape(4, lax.axis_size("tensor"), -1).transpose(1, 0, 2)
    norms = jnp.sum(lax.all_to_all(norms, "tensor", 0, 0, tiled=True), axis=0)
    bias_grad = lax.dynamic_index_in_dim(
        feed_owned[:, dense_end + 2].reshape(lax.axis_size("tensor"), -1), mine, 0, keepdims=False
    )
    return (
        out,
        input_grad,
        norms[0],
        norms[1],
        norms[2],
        norms[3],
        qkv_owned[:, :cols],
        qkv_owned[:bias_own, cols + 2],
        feed_owned[:, down_end:dense_end],
        bias_grad,
        feed_owned[:, :up_end],
        feed_owned[:, dense_end + 3],
        feed_owned[:, up_end:down_end],
        bias_grad,
    )


def solution(mesh):
    placed = (
        P(("dp", "tensor"), None),
        P("dp"),
        P(),
        P(),
        P(),
        P(),
        P("dp", "tensor"),
        P("tensor"),
        P("dp", "tensor"),
        P(),
        P("dp", "tensor"),
        P("tensor"),
        P("dp", "tensor"),
        P(),
        P(("dp", "tensor"), None),
    )
    return jax.shard_map(
        body,
        mesh=mesh,
        in_specs=placed,
        out_specs=(
            P(("dp", "tensor"), None),
            P(("dp", "tensor"), None),
            P(("dp", "tensor")),
            P(("dp", "tensor")),
            P(("dp", "tensor")),
            P(("dp", "tensor")),
            P("dp", "tensor"),
            P(("tensor", "dp")),
            P("dp", "tensor"),
            P(("dp", "tensor")),
            P("dp", "tensor"),
            P(("tensor", "dp")),
            P("dp", "tensor"),
            P(("dp", "tensor")),
        ),
        check_vma=False,
    )
```

```python
import functools

import jax
import jax.numpy as jnp
from jax import lax
from jax.experimental import pallas as pl
from jax.experimental.pallas import tpu as pltpu
from jax.sharding import PartitionSpec as P

HEAD = 64
ROT = 16
HALF = ROT // 2
EPS = 1e-05
NEG = -1e30
SCALE = HEAD ** (-0.5)
WHOLE = 1536
BLOCK = 512
F32 = jnp.float32
BF16 = jnp.bfloat16
VMEM_LIMIT = 56 * 1024 * 1024
MICROSECOND = 1_150_000_000


def dot(left, right):
    return jnp.dot(left, right, preferred_element_type=F32)


def dot_nt(left, right):
    return lax.dot_general(left, right, (((1,), (1,)), ((), ())), preferred_element_type=F32)


def call(kernel, grid, in_specs, out_specs, out_shape, scratch, name, prefetch=0, work=0, aliases={}):
    return pl.pallas_call(
        kernel,
        grid_spec=pltpu.PrefetchScalarGridSpec(
            num_scalar_prefetch=prefetch,
            grid=grid,
            in_specs=in_specs,
            out_specs=out_specs,
            scratch_shapes=scratch,
        ),
        out_shape=out_shape,
        compiler_params=pltpu.CompilerParams(vmem_limit_bytes=VMEM_LIMIT),
        cost_estimate=pl.CostEstimate(flops=work, bytes_accessed=0, transcendentals=0),
        input_output_aliases=aliases,
        name=name,
    )


def whole_spec(shape):
    return pl.BlockSpec(shape, lambda *_: (0,) * len(shape))


def column(ref, index):
    return ref[:, index : index + 1]


def join(pieces, first, count):
    return jnp.concatenate([piece[:, first : first + count] for piece in pieces], axis=0)


def blocks_of(order, rows):
    count = order.shape[0]
    size = rows // count
    return [
        (slice(at * size, (at + 1) * size), pl.ds(pl.multiple_of(order[at] * size, size), size))
        for at in range(count)
    ]


def choose(refs, step, held):
    for index, ref in enumerate(refs):

        @pl.when(step == index)
        def _(ref=ref):
            held[...] = ref[...]

    return held[...]


def fold(values):
    return sum(values[:, at : at + 128] for at in range(0, values.shape[1], 128))


def as_rows(parts, order=None, held=None):
    sums = [jnp.sum(part, axis=1, keepdims=True) for part in parts]
    lane = lax.broadcasted_iota(jnp.int32, parts[0].shape, 1)
    total = jnp.zeros(parts[0].shape, F32)
    for index, item in enumerate(sums):
        total = jnp.where(lane == index, item, total)
    if order is None:
        return total.T[0:8, :]
    return turn_back(order, held, total)[0:8, :]


def kept(items):
    return [pl.BlockSpec(memory_space=pl.ANY) for _ in items]


def standardize(block):
    values = block.astype(F32)
    center = values - jnp.mean(values, axis=0, keepdims=True)
    spread = jnp.mean(center * center, axis=0, keepdims=True)
    return center * lax.rsqrt(spread + EPS)


def turn_kernel(order, rows_ref, *refs):
    out_ref, held = refs[-2:]
    held[...] = rows_ref[...].T
    for here, there in blocks_of(order, out_ref.shape[0]):
        out_ref[here, :] = held[there, :]


def turn(order, rows, wait=()):
    count, width = rows.shape
    part = min(256, count)
    return call(
        turn_kernel,
        (count // part,),
        [pl.BlockSpec((part, width), lambda i, _: (i, 0)), *kept(wait)],
        pl.BlockSpec((width, part), lambda i, _: (0, i)),
        jax.ShapeDtypeStruct((width, count), rows.dtype),
        [pltpu.VMEM((width, part), rows.dtype)],
        "turn",
        prefetch=1,
    )(order, rows, *wait)


def turn_back(order, held, grads):
    for here, there in blocks_of(order, grads.shape[0]):
        held[there, :] = grads[here, :]
    return held[...].T


NORM_ROWS = 4


def stand_kernel(order, rows_ref, *refs):
    out_ref, held = refs[-2:]
    rows = rows_ref[...]
    held[...] = jnp.concatenate([rows, jnp.zeros((128 - rows.shape[0], rows.shape[1]), F32)], axis=0).T
    count = order.shape[0]
    size = rows.shape[1] // count
    lane = lax.broadcasted_iota(jnp.int32, (size, 128), 1)
    for index in range(count):
        first = pl.multiple_of(order[index] * size, size)
        here = slice(index * size, (index + 1) * size)
        out_ref[here, :] = jnp.where(lane < NORM_ROWS, held[pl.ds(first, size), :], held[here, :])


def stand(order, rows, wait):
    shape = (rows.shape[1], 128)
    return call(
        stand_kernel,
        (1,),
        [whole_spec(rows.shape), *kept(wait)],
        whole_spec(shape),
        jax.ShapeDtypeStruct(shape, F32),
        [pltpu.VMEM(shape, F32)],
        "stand",
        prefetch=1,
    )(order, rows, *wait)


def project_kernel(count, place, *refs):
    x_refs, pieces, refs = refs[:4], refs[4 : 4 + count], refs[4 + count :]
    col_ref, cos_ref, sin_ref = refs[:3]
    out_ref, x_now, wt = refs[-3:]
    step = pl.program_id(0)
    cols = out_ref.shape[0]

    @pl.when(step == 0)
    def _():
        wt[...] = join(pieces, 0, cols).T

    unit = standardize(choose(x_refs, step, x_now))
    normed = (unit * column(col_ref, 0) + column(col_ref, 1)).astype(BF16)
    cosine, sine = cos_ref[...], sin_ref[...]
    for head in range(cols // (3 * HEAD)):
        base = head * 3 * HEAD
        mixed = dot(wt[base : base + 3 * HEAD, :], normed) + col_ref[base : base + 3 * HEAD, 5:6]
        for part, factor in ((0, SCALE), (HEAD, 1.0)):
            one, two = mixed[part : part + HALF], mixed[part + HALF : part + ROT]
            turned = jnp.concatenate(
                [one * cosine - two * sine, two * cosine + one * sine, mixed[part + ROT : part + HEAD]],
                axis=0,
            )
            out_ref[base + part : base + part + HEAD, :] = (turned * factor).astype(BF16)
        out_ref[base + 2 * HEAD : base + 3 * HEAD, :] = mixed[2 * HEAD :].astype(BF16)


def project(place, x_all, pieces, columns, cosine, sine, wait):
    width, slab = x_all[0].shape
    cols = pieces[0].shape[1]
    by_place = lambda s, t: (0, s ^ t[0])
    return call(
        functools.partial(project_kernel, len(pieces)),
        (len(x_all),),
        [whole_spec(item.shape) for item in (*x_all, *pieces, columns)]
        + [pl.BlockSpec((HALF, slab), by_place), pl.BlockSpec((HALF, slab), by_place), *kept(wait)],
        pl.BlockSpec((cols, slab), by_place),
        jax.ShapeDtypeStruct((cols, len(x_all) * slab), BF16),
        [pltpu.VMEM((width, slab), BF16), pltpu.VMEM((cols, width), BF16)],
        "project",
        prefetch=1,
        work=1 * MICROSECOND,
    )(place, *x_all, *pieces, columns, cosine, sine, *wait)


def masked(scores, first_key, first_query, starts):
    diagonal = first_key + scores.shape[0] > first_query
    ragged = first_query + scores.shape[1] > WHOLE
    if not (diagonal or ragged):
        return scores
    key = first_key + lax.broadcasted_iota(jnp.int32, scores.shape, 0)
    allowed = key >= starts
    if diagonal:
        allowed &= key <= first_query + lax.broadcasted_iota(jnp.int32, scores.shape, 1)
    return jnp.where(allowed, scores, NEG)


def attend_kernel(handed, start_ref, qkv_ref, *refs):
    out_ref, lse_ref = refs[-4 - handed : len(refs) - 2 - handed]
    keys, held = refs[-2:]
    rows = qkv_ref.shape[1]
    block = min(BLOCK, rows)
    keys[...] = qkv_ref[HEAD : 2 * HEAD, :].T
    for begin in range(0, rows, block):
        here = slice(begin, begin + block)
        queries, starts = qkv_ref[0:HEAD, here], start_ref[0:1, here]
        top = jnp.full((1, block), NEG, F32)
        for first in range(0, begin + block, block):
            scores = masked(dot(keys[first : first + block, :], queries), first, begin, starts)
            held[first : first + block, :] = scores
            top = jnp.maximum(top, jnp.max(scores, axis=0, keepdims=True))
        total = jnp.zeros((1, block), F32)
        result = jnp.zeros((HEAD, block), F32)
        for first in range(0, begin + block, block):
            expo = jnp.exp(held[first : first + block, :] - top)
            total += jnp.sum(expo, axis=0, keepdims=True)
            result += dot(qkv_ref[2 * HEAD : 3 * HEAD, first : first + block], expo.astype(BF16))
        out_ref[:, here] = (result / total).astype(BF16)
        lse_ref[0, 0:1, here] = top + jnp.log(total)


def attend(starts, qkv, first, heads, wait, through):
    rows = qkv.shape[1]
    return call(
        functools.partial(attend_kernel, len(through)),
        (heads,),
        [whole_spec(starts.shape), pl.BlockSpec((3 * HEAD, rows), lambda h: (h + first, 0))]
        + kept((*through, *wait)),
        [pl.BlockSpec((HEAD, rows), lambda h: (h, 0)), pl.BlockSpec((1, 1, rows), lambda h: (h, 0, 0))]
        + kept(through),
        [jax.ShapeDtypeStruct((heads * HEAD, rows), BF16), jax.ShapeDtypeStruct((heads, 1, rows), F32)]
        + [jax.ShapeDtypeStruct(item.shape, item.dtype) for item in through],
        [pltpu.VMEM((rows, HEAD), BF16), pltpu.VMEM((rows, min(BLOCK, rows)), F32)],
        "attend",
        work=heads * MICROSECOND,
        aliases={2 + index: 2 + index for index in range(len(through))},
    )(starts, qkv, *through, *wait)


def attend_back_kernel(start_ref, cos_ref, sin_ref, qkv_ref, grad_ref, out_ref, lse_ref, *refs):
    mixed_ref, keys, values, key_sum, value_sum = refs[-5:]
    rows = qkv_ref.shape[1]
    block = min(BLOCK, rows)
    keys[...] = qkv_ref[HEAD : 2 * HEAD, :].T
    values[...] = qkv_ref[2 * HEAD : 3 * HEAD, :].T
    key_sum[...] = jnp.zeros_like(key_sum)
    value_sum[...] = jnp.zeros_like(value_sum)

    def put_unrotated(base, here, grads):
        cosine, sine = cos_ref[:, here], sin_ref[:, here]
        one, two = grads[0:HALF, :], grads[HALF:ROT, :]
        turned = jnp.concatenate(
            [one * cosine + two * sine, two * cosine - one * sine, grads[ROT:, :]], axis=0
        )
        mixed_ref[base : base + HEAD, here] = turned.astype(BF16)

    for begin in range(0, rows, block):
        here = slice(begin, begin + block)
        queries, grads, starts = qkv_ref[0:HEAD, here], grad_ref[:, here], start_ref[0:1, here]
        lse = lse_ref[0, 0:1, here]
        inner = jnp.sum(grads.astype(F32) * out_ref[:, here].astype(F32), axis=0, keepdims=True)
        query_rows, grad_rows = queries.T, grads.T
        query_sum = jnp.zeros((HEAD, block), F32)
        for first in range(0, begin + block, block):
            there = slice(first, first + block)
            scores = masked(dot(keys[there, :], queries), first, begin, starts)
            probs = jnp.exp(scores - lse)
            score_grads = (probs * (dot(values[there, :], grads) - inner)).astype(BF16)
            query_sum += dot(qkv_ref[HEAD : 2 * HEAD, there], score_grads)
            key_sum[there, :] += dot(score_grads, query_rows)
            value_sum[there, :] += dot(probs.astype(BF16), grad_rows)
        put_unrotated(0, here, query_sum * SCALE)
    put_unrotated(HEAD, slice(0, rows), key_sum[...].T)
    mixed_ref[2 * HEAD : 3 * HEAD, :] = value_sum[...].T.astype(BF16)


def attend_back(starts, cosine, sine, qkv, grads, out, lse, first, wait):
    rows = qkv.shape[1]
    heads = lse.shape[0]
    return call(
        attend_back_kernel,
        (heads,),
        [
            whole_spec(starts.shape),
            whole_spec(cosine.shape),
            whole_spec(sine.shape),
            pl.BlockSpec((3 * HEAD, rows), lambda h: (h + first, 0)),
            pl.BlockSpec((HEAD, rows), lambda h: (h + first, 0)),
            pl.BlockSpec((HEAD, rows), lambda h: (h, 0)),
            pl.BlockSpec((1, 1, rows), lambda h: (h, 0, 0)),
            *kept(wait),
        ],
        pl.BlockSpec((3 * HEAD, rows), lambda h: (h, 0)),
        jax.ShapeDtypeStruct((heads * 3 * HEAD, rows), BF16),
        [pltpu.VMEM((rows, HEAD), BF16)] * 2 + [pltpu.VMEM((rows, HEAD), F32)] * 2,
        "attend_back",
        work=9 * heads * MICROSECOND,
    )(starts, cosine, sine, qkv, grads, out, lse, *wait)


def feed_kernel(place, order, *refs):
    x_refs, dy_refs, refs = refs[:4], refs[4:8], refs[8:]
    weight_ref, att_refs, refs = refs[0], refs[1:-22], refs[-22:]
    col_ref, *refs = refs
    branch_refs, (normed_ref, att_grad_ref, weights_ref, vector_ref), refs = refs[:4], refs[4:8], refs[8:]
    x_now, dy_now, up, down, dense, up_t, down_t, dense_t, active, hidden_grad, sums, vectors, held = refs
    step = pl.program_id(0)
    hidden_count = up.shape[1]
    dense_count = dense.shape[1]

    @pl.when(step == 0)
    def _():
        for here, there in blocks_of(order, up.shape[0]):
            up[here, :] = weight_ref[there, :hidden_count]
            down[here, :] = weight_ref[there, hidden_count : 2 * hidden_count]
            dense[here, :] = weight_ref[there, 2 * hidden_count :]
        up_t[...] = up[...].T
        down_t[...] = down[...].T
        dense_t[...] = dense[...].T
        sums[...] = jnp.zeros_like(sums)
        vectors[...] = jnp.zeros_like(vectors)

    unit = standardize(choose(x_refs, step, x_now))
    dy = choose(dy_refs, step, dy_now)
    normed = (unit * column(col_ref, 2) + column(col_ref, 3)).astype(BF16)
    attended = jnp.concatenate([ref[...] for ref in att_refs], axis=0)
    att_grad_ref[...] = dot(dense_t[...], dy).astype(BF16)
    chunk = min(256, hidden_count)
    for first in range(0, hidden_count, chunk):
        units = slice(first, first + chunk)
        hidden = dot(up_t[units, :], normed) + col_ref[units, 4:5]
        chance = 0.5 + 0.5 * lax.erf(hidden * (0.5**0.5))
        density = jnp.exp(hidden * hidden * -0.5) * (hidden * 0.3989422804014327)
        now = (hidden * chance).astype(BF16)
        back = (dot(down_t[units, :], dy) * (chance + density)).astype(BF16)
        active[units, :] = now
        hidden_grad[units, :] = back
        sums[:, units] += dot_nt(normed, back)
        sums[:, hidden_count + first : hidden_count + first + chunk] += dot_nt(dy, now)
        vectors[3, units, :] += fold(back.astype(F32))
    sums[:, 2 * hidden_count :] += dot_nt(dy, attended)
    branch = (dot(dense[...], attended) + dot(down[...], active[...])).astype(BF16)
    for index, ref in enumerate(branch_refs):

        @pl.when(step == index)
        def _(ref=ref):
            ref[...] = branch

    normed_grad = dot(up[...], hidden_grad[...])
    normed_ref[0] = normed_grad * column(col_ref, 2)
    vectors[0] += fold(normed_grad * unit)
    vectors[1] += fold(normed_grad)
    vectors[2] += fold(dy.astype(F32))

    @pl.when(step == pl.num_programs(0) - 1)
    def _():
        for here, there in blocks_of(order, sums.shape[0]):
            weights_ref[there, :] = sums[here, :].astype(BF16)
        rows = as_rows([vectors[0], vectors[1], vectors[2]], order, held)
        vector_ref[...] = jnp.concatenate([rows[0:3], as_rows([vectors[3]])[0:5]], axis=0)


def feed(place, order, x_all, dy_all, weights, attended, columns):
    width, slab = x_all[0].shape
    parts = len(x_all)
    dense_count = sum(item.shape[0] for item in attended)
    hidden_count = (weights.shape[1] - dense_count) // 2
    grad_cols = 2 * hidden_count + dense_count
    by_place = lambda s, t, _: (0, s ^ t[0])
    return call(
        feed_kernel,
        (parts,),
        [whole_spec(item.shape) for item in (*x_all, *dy_all, weights)]
        + [pl.BlockSpec((item.shape[0], slab), by_place) for item in attended]
        + [whole_spec(columns.shape)],
        [whole_spec((width, slab))] * parts
        + [
            pl.BlockSpec((1, width, slab), lambda s, *_: (s, 0, 0)),
            pl.BlockSpec((dense_count, slab), by_place),
            whole_spec((width, grad_cols)),
            whole_spec((8, hidden_count)),
        ],
        [jax.ShapeDtypeStruct((width, slab), BF16)] * parts
        + [
            jax.ShapeDtypeStruct((parts, width, slab), F32),
            jax.ShapeDtypeStruct((dense_count, parts * slab), BF16),
            jax.ShapeDtypeStruct((width, grad_cols), BF16),
            jax.ShapeDtypeStruct((8, hidden_count), F32),
        ],
        [
            pltpu.VMEM((width, slab), BF16),
            pltpu.VMEM((width, slab), BF16),
            pltpu.VMEM((width, hidden_count), BF16),
            pltpu.VMEM((width, hidden_count), BF16),
            pltpu.VMEM((width, dense_count), BF16),
            pltpu.VMEM((hidden_count, width), BF16),
            pltpu.VMEM((hidden_count, width), BF16),
            pltpu.VMEM((dense_count, width), BF16),
            pltpu.VMEM((hidden_count, slab), BF16),
            pltpu.VMEM((hidden_count, slab), BF16),
            pltpu.VMEM((width, grad_cols), F32),
            pltpu.VMEM((4, hidden_count, 128), F32),
            pltpu.VMEM((width, 128), F32),
        ],
        "feed",
        prefetch=2,
        work=30 * MICROSECOND,
    )(place, order, *x_all, *dy_all, weights, *attended, columns)


def project_back_kernel(count, heads, place, order, *refs):
    x_refs, pieces, refs = refs[:4], refs[4 : 4 + count], refs[4 + count :]
    mixed_refs, refs = refs[:heads], refs[heads:]
    part_ref, col_ref, refs = refs[0], refs[1], refs[-13:]
    unit_refs, (own_ref, sent_ref, vector_ref), refs = refs[:4], refs[4:7], refs[7:]
    x_now, w, sums, vectors, counts, held = refs
    step = pl.program_id(0)

    @pl.when(step == 0)
    def _():
        w[...] = join(pieces, 0, w.shape[1])
        sums[...] = jnp.zeros_like(sums)
        vectors[...] = jnp.zeros_like(vectors)
        counts[...] = jnp.zeros_like(counts)

    unit = standardize(choose(x_refs, step, x_now))
    normed = (unit * column(col_ref, 0) + column(col_ref, 1)).astype(BF16)
    mixed = jnp.concatenate([ref[...] for ref in mixed_refs], axis=0)
    sums[...] += dot_nt(normed, mixed)
    counts[...] += fold(mixed.astype(F32))
    normed_grad = dot(w[...], mixed)
    total = (part_ref[0] + normed_grad * column(col_ref, 0)).astype(BF16)
    for index, ref in enumerate(unit_refs):

        @pl.when(step == index)
        def _(ref=ref):
            ref[...] = total

    vectors[0] += fold(normed_grad * unit)
    vectors[1] += fold(normed_grad)

    @pl.when(step == pl.num_programs(0) - 1)
    def _():
        half = own_ref.shape[0]
        own_ref[...] = sums[:half, :].astype(BF16)
        sent_ref[...] = sums[half:, :].astype(BF16)
        rows = as_rows([vectors[0], vectors[1]], order, held)
        tail = as_rows([counts[...]])[0:6]
        tail = jnp.concatenate([tail, jnp.zeros((6, rows.shape[1] - tail.shape[1]), F32)], axis=1)
        vector_ref[...] = jnp.concatenate([rows[0:2], tail], axis=0)


def project_back(place, order, x_all, pieces, mixed, part, columns, wait):
    width, slab = x_all[0].shape
    parts = len(x_all)
    cols = sum(item.shape[0] for item in mixed)
    return call(
        functools.partial(project_back_kernel, len(pieces), len(mixed)),
        (parts,),
        [whole_spec(item.shape) for item in (*x_all, *pieces)]
        + [pl.BlockSpec((item.shape[0], slab), lambda s, t, _: (0, s ^ t[0])) for item in mixed]
        + [pl.BlockSpec((1, width, slab), lambda s, *_: (s, 0, 0)), whole_spec(columns.shape)]
        + kept(wait),
        [whole_spec((width, slab))] * parts
        + [
            whole_spec((width // 2, cols)),
            whole_spec((width // 2, cols)),
            whole_spec((8, width)),
        ],
        [jax.ShapeDtypeStruct((width, slab), BF16)] * parts
        + [
            jax.ShapeDtypeStruct((width // 2, cols), BF16),
            jax.ShapeDtypeStruct((width // 2, cols), BF16),
            jax.ShapeDtypeStruct((8, width), F32),
        ],
        [
            pltpu.VMEM((width, slab), BF16),
            pltpu.VMEM((width, cols), BF16),
            pltpu.VMEM((width, cols), F32),
            pltpu.VMEM((2, width, 128), F32),
            pltpu.VMEM((cols, 128), F32),
            pltpu.VMEM((width, 128), F32),
        ],
        "project_back",
        prefetch=2,
        work=13 * MICROSECOND,
    )(place, order, *x_all, *pieces, *mixed, part, columns, *wait)


def finish_out_kernel(order, own_ref, near_ref, far_ref, rows_ref, bias_ref, *refs):
    out_ref, held = refs[-2:]
    branch = own_ref[...].astype(F32) + near_ref[...].astype(F32) + far_ref[...].astype(F32)
    branch = turn_back(order, held, branch)
    out_ref[...] = (rows_ref[...].astype(F32) + branch + bias_ref[...]).astype(BF16)


def finish(kernel, order, summands, rows, others, kind, name, work, wait=()):
    count, width = rows.shape
    part = min(128, count)
    rows_block = pl.BlockSpec((part, width), lambda i, _: (i, 0))
    return call(
        kernel,
        (count // part,),
        [pl.BlockSpec((width, part), lambda i, _: (0, i))] * len(summands)
        + [rows_block]
        + [rows_block if item.shape == rows.shape else whole_spec(item.shape) for item in others]
        + kept(wait),
        rows_block,
        jax.ShapeDtypeStruct(rows.shape, kind),
        [pltpu.VMEM((width, part), F32)],
        name,
        prefetch=1,
        work=work * MICROSECOND,
    )(order, *summands, rows, *others, *wait)


def finish_grad_kernel(order, own_ref, near_ref, far_ref, rows_ref, dy_ref, out_ref, held):
    grads = own_ref[...].astype(F32) + near_ref[...].astype(F32) + far_ref[...].astype(F32)
    grads = turn_back(order, held, grads)
    rows = rows_ref[...].astype(F32)
    center = rows - jnp.mean(rows, axis=1, keepdims=True)
    scale = lax.rsqrt(jnp.mean(center * center, axis=1, keepdims=True) + EPS)
    unit = center * scale
    along = jnp.mean(grads * unit, axis=1, keepdims=True)
    level = jnp.mean(grads, axis=1, keepdims=True)
    out_ref[...] = dy_ref[...].astype(F32) + scale * (grads - level - unit * along)


def share_kernel(own_ref, near_ref, last_ref, first_ref, *refs):
    far_ref, norms_ref, others_ref = refs[-3:]
    far_ref[...] = (own_ref[...].astype(F32) + near_ref[...].astype(F32)).astype(BF16)
    norms_ref[...] = jnp.concatenate([last_ref[0:2, :], first_ref[0:2, :]], axis=0)
    others_ref[...] = jnp.concatenate([first_ref[2:4, :], last_ref[2:4, :]], axis=0)


def share(own, near, last, first, wait):
    pair = (4, last.shape[1])
    return call(
        share_kernel,
        (1,),
        [whole_spec(item.shape) for item in (own, near, last, first)] + kept(wait),
        [whole_spec(own.shape), whole_spec(pair), whole_spec(pair)],
        [jax.ShapeDtypeStruct(own.shape, BF16), jax.ShapeDtypeStruct(pair, F32), jax.ShapeDtypeStruct(pair, F32)],
        [],
        "share",
        work=1 * MICROSECOND,
    )(own, near, last, first, *wait)


def halve_kernel(own_ref, came_ref, *refs):
    outs = refs[-4:]
    size = outs[0].shape[0]
    for index, ref in enumerate(outs):
        rows = slice(index * size, (index + 1) * size)
        ref[...] = (own_ref[rows, :].astype(F32) + came_ref[rows, :].astype(F32)).astype(ref.dtype)


def halve(own, came, wait, work=2):
    shape = (own.shape[0] // 4, own.shape[1])
    return call(
        halve_kernel,
        (1,),
        [whole_spec(own.shape), whole_spec(came.shape), *kept(wait)],
        [whole_spec(shape)] * 4,
        [jax.ShapeDtypeStruct(shape, kind) for kind in (F32, BF16, BF16, BF16)],
        [],
        "halve",
        work=work * MICROSECOND,
    )(own, came, *wait)


def total_kernel(kept_ref, *refs):
    came, (kept_rows, *came_rows), refs = refs[:3], refs[3:7], refs[7:]
    out_ref, rows_ref = refs[-2:]
    out_ref[...] = kept_ref[...] + sum(ref[...].astype(F32) for ref in came)
    rows_ref[...] = kept_rows[...] + sum(ref[...] for ref in came_rows)


def total(items, rows, wait):
    return call(
        total_kernel,
        (1,),
        [whole_spec(item.shape) for item in (*items, *rows)] + kept(wait),
        [whole_spec(items[0].shape), whole_spec(rows[0].shape)],
        [jax.ShapeDtypeStruct(items[0].shape, F32), jax.ShapeDtypeStruct(rows[0].shape, F32)],
        [],
        "total",
        work=1 * MICROSECOND,
    )(*items, *rows, *wait)


def gate_kernel(*refs):
    pass


def gate(item, wait):
    return call(
        gate_kernel,
        (1,),
        kept((item, *wait)),
        kept((item,))[0],
        jax.ShapeDtypeStruct(item.shape, item.dtype),
        [],
        "gate",
        aliases={0: 0},
    )(item, *wait)


def swap(value, axis, bits):
    count = lax.axis_size(axis)
    return lax.ppermute(value, axis, [(i, i ^ bits) for i in range(count)])


def gather_group(own):
    far = swap(own, "tensor", 2)
    near = swap(own, "tensor", 1)
    return (own, near, far, swap(far, "tensor", 1))


def scatter_group(slabs):
    far = (slabs[2].astype(F32) + swap(slabs[3], "tensor", 1).astype(F32)).astype(BF16)
    return (slabs[0], swap(slabs[1], "tensor", 1), swap(far, "tensor", 2)), (far,)


PARTNERS = (0, 2, 4, 6, 1, 3, 5, 7)


def paired():
    return lax.axis_size("dp") == len(PARTNERS)


def feature_order():
    if paired():
        return jnp.array(PARTNERS, jnp.int32) ^ lax.axis_index("dp").astype(jnp.int32)
    return jnp.zeros((1,), jnp.int32)


def gather_rows(own):
    if not paired():
        return (lax.all_gather(own, "dp", axis=0, tiled=True),)
    same = [own] + [swap(own, "dp", bits) for bits in PARTNERS[1:4]]
    return (*same, *(swap(piece, "dp", 1) for piece in same))


def partner_sums(own, sent):
    kept_block, *outward = halve(own, swap(sent, "dp", 1), ())
    return (kept_block, *(swap(half, "dp", bits) for half, bits in zip(outward, PARTNERS[1:4])))


def vector_sums(norms, others):
    norms = norms + swap(norms, "tensor", 1) + swap(norms, "tensor", 2) + swap(norms, "tensor", 3)
    rows = jnp.concatenate([norms, others], axis=0)
    rows = rows + swap(rows, "dp", 1)
    return (rows, *(swap(rows, "dp", bits) for bits in PARTNERS[1:4]))


def body(
    tokens,
    segment_ids,
    ln1_gain,
    ln1_bias,
    ln2_gain,
    ln2_bias,
    w_qkv,
    b_qkv,
    w_dense,
    b_dense,
    w_fc1,
    b_fc1,
    w_fc2,
    b_fc2,
    cotangent,
):
    group_rows = segment_ids.shape[0]
    width = tokens.shape[1]
    own_width = w_qkv.shape[0]
    dp_count = lax.axis_size("dp")
    tensor_count = lax.axis_size("tensor")
    mine = lax.axis_index("tensor").astype(jnp.int32)
    place = mine.reshape(1)
    order = feature_order()

    firsts = gather_rows(w_qkv)
    x_all = gather_group(turn(order, tokens))
    weights = lax.all_gather(jnp.concatenate([w_fc1, w_fc2, w_dense], axis=1), "dp", axis=0, tiled=True)
    rows = jnp.stack([ln1_gain, ln1_bias, ln2_gain, ln2_bias, b_fc1, jnp.pad(b_qkv, (0, width - b_qkv.shape[0]))])
    columns = stand(order, jnp.pad(rows, ((0, 2), (0, 0))), ())
    dy_own = gate(turn(order, cotangent), (x_all[2], *firsts[4:]))
    dy_far, dy_near = swap(dy_own, "tensor", 2), swap(dy_own, "tensor", 1)

    row = jnp.arange(group_rows, dtype=jnp.int32)
    padding = segment_ids != segment_ids[0]
    length = jnp.sum(jnp.where(padding, 0, 1))
    starts = jnp.where(padding, length, 0)
    inverse = 10000.0 ** (-jnp.arange(0, ROT, 2, dtype=F32) / ROT)
    angles = inverse[:, None] * (row - starts).astype(F32)[None, :]
    cosine, sine = jnp.cos(angles), jnp.sin(angles)
    starts = starts[None, :]

    qkv = project(place, x_all, firsts, columns, cosine, sine, (dy_own,))
    heads = range(qkv.shape[0] // (3 * HEAD))
    attended, lse = [], []
    for head in heads:
        through = (dy_far,) if head == 1 else ()
        result, scale, *through = attend(starts, qkv, head, 1, attended[-1:], through)
        attended.append(result)
        lse.append(scale)
        if head == 1:
            (dy_far,) = through
    dy_all = (dy_own, dy_near, dy_far, swap(dy_far, "tensor", 1))
    *branch, part, att_grad, feed_grads, feed_vectors = feed(
        place, order, x_all, dy_all, weights, attended, columns
    )
    feed_grads = lax.psum_scatter(feed_grads, "dp", scatter_dimension=0, tiled=True).astype(F32)
    out_summands, branch_wait = scatter_group(branch)

    mixed_grad = []
    for head in heads:
        wait = (*branch_wait, *mixed_grad[-1:]) if head == 1 else mixed_grad[-1:]
        mixed_grad.append(
            attend_back(starts, cosine, sine, qkv, att_grad, attended[head], lse[head], head, wait)
        )
    *unit_grad, qkv_own, qkv_sent, last_vectors = project_back(
        place, order, x_all, firsts, mixed_grad, part, columns, out_summands[2:]
    )
    far, norms, others = share(
        unit_grad[2], swap(unit_grad[3], "tensor", 1), last_vectors, feed_vectors, ()
    )
    summands = (unit_grad[0], swap(unit_grad[1], "tensor", 1), swap(far, "tensor", 2))
    input_grad = finish(
        finish_grad_kernel, order, summands, tokens, (cotangent,), F32, "finish_grad", 5
    )
    bias = (b_dense + b_fc2)[None, :]
    out = finish(
        finish_out_kernel, order, out_summands, tokens, (bias,), BF16, "finish_out", 4, (input_grad,)
    )
    if paired():
        qkv_grads, vectors = total(
            partner_sums(qkv_own, qkv_sent), vector_sums(norms, others), (input_grad,)
        )
    else:
        qkv_grads = jnp.concatenate([qkv_own, qkv_sent], axis=0)
        qkv_grads = lax.psum_scatter(qkv_grads, "dp", scatter_dimension=0, tiled=True).astype(F32)
        vectors = lax.psum(jnp.concatenate([lax.psum(norms, "tensor"), others], axis=0), "dp")
    at = lax.axis_index("dp") * own_width + mine * (own_width // tensor_count)
    norm_grads = lax.dynamic_slice_in_dim(vectors[:5], at, own_width // tensor_count, 1)
    hidden_bias = lax.dynamic_slice_in_dim(vectors[5], lax.axis_index("dp") * own_width, own_width, 0)
    bias_own = b_qkv.shape[0] // dp_count
    qkv_bias = lax.dynamic_slice_in_dim(vectors[6], lax.axis_index("dp") * bias_own, bias_own, 0)
    hidden_count = w_fc1.shape[1]
    return (
        out,
        input_grad,
        norm_grads[0],
        norm_grads[1],
        norm_grads[2],
        norm_grads[3],
        qkv_grads,
        qkv_bias,
        feed_grads[:, 2 * hidden_count :],
        norm_grads[4],
        feed_grads[:, :hidden_count],
        hidden_bias,
        feed_grads[:, hidden_count : 2 * hidden_count],
        norm_grads[4],
    )


def solution(mesh):
    placed = (
        P(("dp", "tensor"), None),
        P("dp"),
        P(),
        P(),
        P(),
        P(),
        P("dp", "tensor"),
        P("tensor"),
        P("dp", "tensor"),
        P(),
        P("dp", "tensor"),
        P("tensor"),
        P("dp", "tensor"),
        P(),
        P(("dp", "tensor"), None),
    )
    return jax.shard_map(
        body,
        mesh=mesh,
        in_specs=placed,
        out_specs=(
            P(("dp", "tensor"), None),
            P(("dp", "tensor"), None),
            P(("dp", "tensor")),
            P(("dp", "tensor")),
            P(("dp", "tensor")),
            P(("dp", "tensor")),
            P("dp", "tensor"),
            P(("tensor", "dp")),
            P("dp", "tensor"),
            P(("dp", "tensor")),
            P("dp", "tensor"),
            P(("tensor", "dp")),
            P("dp", "tensor"),
            P(("dp", "tensor")),
        ),
        check_vma=False,
    )
```

```python
import functools

import jax
import jax.numpy as jnp
from jax import lax
from jax.experimental import pallas as pl
from jax.experimental.pallas import tpu as pltpu
from jax.sharding import PartitionSpec as P

HEAD = 64
ROT = 16
HALF = ROT // 2
EPS = 1e-05
NEG = -1e30
SCALE = HEAD ** (-0.5)
WHOLE = 1536
BLOCK = 512
F32 = jnp.float32
BF16 = jnp.bfloat16
VMEM_LIMIT = 56 * 1024 * 1024
MICROSECOND = 1_150_000_000
CHUNK = 768


def dot(left, right):
    return jnp.dot(left, right, preferred_element_type=F32)


def dot_nt(left, right):
    return lax.dot_general(left, right, (((1,), (1,)), ((), ())), preferred_element_type=F32)


def call(kernel, grid, in_specs, out_specs, out_shape, scratch, name, prefetch=0, work=0, aliases={}):
    return pl.pallas_call(
        kernel,
        grid_spec=pltpu.PrefetchScalarGridSpec(
            num_scalar_prefetch=prefetch,
            grid=grid,
            in_specs=in_specs,
            out_specs=out_specs,
            scratch_shapes=scratch,
        ),
        out_shape=out_shape,
        compiler_params=pltpu.CompilerParams(vmem_limit_bytes=VMEM_LIMIT),
        cost_estimate=pl.CostEstimate(flops=work, bytes_accessed=0, transcendentals=0),
        input_output_aliases=aliases,
        name=name,
    )


def whole_spec(shape):
    return pl.BlockSpec(shape, lambda *_: (0,) * len(shape))


def column(ref, index):
    return ref[:, index : index + 1]


def join(pieces, first, count):
    return jnp.concatenate([piece[:, first : first + count] for piece in pieces], axis=0)


def blocks_of(order, rows):
    count = order.shape[0]
    size = rows // count
    return [
        (slice(at * size, (at + 1) * size), pl.ds(pl.multiple_of(order[at] * size, size), size))
        for at in range(count)
    ]


def choose(refs, step, held):
    for index, ref in enumerate(refs):

        @pl.when(step == index)
        def _(ref=ref):
            held[...] = ref[...]

    return held[...]


def fold(values):
    return sum(values[:, at : at + 128] for at in range(0, values.shape[1], 128))


def as_rows(parts, order=None, held=None):
    sums = [jnp.sum(part, axis=1, keepdims=True) for part in parts]
    lane = lax.broadcasted_iota(jnp.int32, parts[0].shape, 1)
    total = jnp.zeros(parts[0].shape, F32)
    for index, item in enumerate(sums):
        total = jnp.where(lane == index, item, total)
    if order is None:
        return total.T[0:8, :]
    return turn_back(order, held, total)[0:8, :]


def by_unit(along, level, col_ref, index):
    return (along - level * column(col_ref, index + 1)) / column(col_ref, index)


def kept(items):
    return [pl.BlockSpec(memory_space=pl.ANY) for _ in items]


def standardize(block):
    values = block.astype(F32)
    center = values - jnp.mean(values, axis=0, keepdims=True)
    spread = jnp.mean(center * center, axis=0, keepdims=True)
    return center * lax.rsqrt(spread + EPS)


def turn_kernel(order, rows_ref, *refs):
    out_ref, held = refs[-2:]
    held[...] = rows_ref[...].T
    for here, there in blocks_of(order, out_ref.shape[0]):
        out_ref[here, :] = held[there, :]


def turn(order, rows, wait=()):
    count, width = rows.shape
    part = min(256, count)
    return call(
        turn_kernel,
        (count // part,),
        [pl.BlockSpec((part, width), lambda i, _: (i, 0)), *kept(wait)],
        pl.BlockSpec((width, part), lambda i, _: (0, i)),
        jax.ShapeDtypeStruct((width, count), rows.dtype),
        [pltpu.VMEM((width, part), rows.dtype)],
        "turn",
        prefetch=1,
    )(order, rows, *wait)


def turn_back(order, held, grads):
    for here, there in blocks_of(order, grads.shape[0]):
        held[there, :] = grads[here, :]
    return held[...].T


def stand_kernel(order, rows_ref, *refs):
    out_ref, held = refs[-2:]
    rows = rows_ref[...]
    held[...] = jnp.concatenate([rows, jnp.zeros((128 - rows.shape[0], rows.shape[1]), F32)], axis=0).T
    count = order.shape[0]
    size = rows.shape[1] // count
    lane = lax.broadcasted_iota(jnp.int32, (size, 128), 1)
    for index in range(count):
        first = pl.multiple_of(order[index] * size, size)
        here = slice(index * size, (index + 1) * size)
        out_ref[here, :] = jnp.where((lane < 4) | (lane == 6), held[pl.ds(first, size), :], held[here, :])


def stand(order, rows, wait):
    shape = (rows.shape[1], 128)
    return call(
        stand_kernel,
        (1,),
        [whole_spec(rows.shape), *kept(wait)],
        whole_spec(shape),
        jax.ShapeDtypeStruct(shape, F32),
        [pltpu.VMEM(shape, F32)],
        "stand",
        prefetch=1,
    )(order, rows, *wait)


def project_kernel(count, place, *refs):
    x_refs, pieces, refs = refs[:4], refs[4 : 4 + count], refs[4 + count :]
    col_ref, cos_ref, sin_ref = refs[:3]
    out_ref, one_ref, two_ref, x_now, wt = refs[-5:]
    step = pl.program_id(0)
    cols = out_ref.shape[0]

    @pl.when(step == 0)
    def _():
        wt[...] = join(pieces, 0, cols).T

    unit = standardize(choose(x_refs, step, x_now))
    normed = (unit * column(col_ref, 0) + column(col_ref, 1)).astype(BF16)
    one_ref[0] = normed
    two_ref[0] = (unit * column(col_ref, 2) + column(col_ref, 3)).astype(BF16)
    cosine, sine = cos_ref[...], sin_ref[...]
    joined = dot(wt[...], normed) + col_ref[:cols, 5:6]
    for head in range(cols // (3 * HEAD)):
        base = head * 3 * HEAD
        mixed = joined[base : base + 3 * HEAD, :]
        for part, factor in ((0, SCALE), (HEAD, 1.0)):
            one, two = mixed[part : part + HALF], mixed[part + HALF : part + ROT]
            turned = jnp.concatenate(
                [one * cosine - two * sine, two * cosine + one * sine, mixed[part + ROT : part + HEAD]],
                axis=0,
            )
            out_ref[base + part : base + part + HEAD, :] = (turned * factor).astype(BF16)
        out_ref[base + 2 * HEAD : base + 3 * HEAD, :] = mixed[2 * HEAD :].astype(BF16)


def project(place, x_all, pieces, columns, cosine, sine, wait):
    width, slab = x_all[0].shape
    cols = pieces[0].shape[1]
    by_place = lambda s, t: (0, s ^ t[0])
    return call(
        functools.partial(project_kernel, len(pieces)),
        (len(x_all),),
        [whole_spec(item.shape) for item in (*x_all, *pieces, columns)]
        + [pl.BlockSpec((HALF, slab), by_place), pl.BlockSpec((HALF, slab), by_place), *kept(wait)],
        [
            pl.BlockSpec((cols, slab), by_place),
            pl.BlockSpec((1, width, slab), lambda s, t: (s, 0, 0)),
            pl.BlockSpec((1, width, slab), lambda s, t: (s, 0, 0)),
        ],
        [
            jax.ShapeDtypeStruct((cols, len(x_all) * slab), BF16),
            jax.ShapeDtypeStruct((len(x_all), width, slab), BF16),
            jax.ShapeDtypeStruct((len(x_all), width, slab), BF16),
        ],
        [pltpu.VMEM((width, slab), BF16), pltpu.VMEM((cols, width), BF16)],
        "project",
        prefetch=1,
        work=1 * MICROSECOND,
    )(place, *x_all, *pieces, columns, cosine, sine, *wait)


def masked(scores, first_key, first_query, starts):
    diagonal = first_key + scores.shape[0] > first_query
    ragged = first_query + scores.shape[1] > WHOLE
    if not (diagonal or ragged):
        return scores
    key = first_key + lax.broadcasted_iota(jnp.int32, scores.shape, 0)
    allowed = key >= starts
    if diagonal:
        allowed &= key <= first_query + lax.broadcasted_iota(jnp.int32, scores.shape, 1)
    return jnp.where(allowed, scores, NEG)


def key_parts(begin, block):
    half = block // 2
    parts = [(first, block, 0) for first in range(0, begin, block)]
    return parts + [(begin, half, 0), (begin + half, half, half)]


def widen(values, skip, fill):
    if not skip:
        return values
    return jnp.concatenate([jnp.full((values.shape[0], skip), fill, values.dtype), values], axis=1)


def attend_kernel(handed, start_ref, qkv_ref, *refs):
    out_ref, lse_ref = refs[-4 - handed : len(refs) - 2 - handed]
    keys, held = refs[-2:]
    rows = qkv_ref.shape[1]
    block = min(BLOCK, rows)
    keys[...] = qkv_ref[HEAD : 2 * HEAD, :].T
    for begin in range(0, rows, block):
        here = slice(begin, begin + block)
        queries, starts = qkv_ref[0:HEAD, here], start_ref[0:1, here]
        top = jnp.full((1, block), NEG, F32)
        for first, count, skip in key_parts(begin, block):
            scores = masked(dot(keys[first : first + count, :], queries[:, skip:]), first, begin + skip, starts[:, skip:])
            held[first : first + count, skip:] = scores
            top = jnp.maximum(top, widen(jnp.max(scores, axis=0, keepdims=True), skip, NEG))
        total = jnp.zeros((1, block), F32)
        result = jnp.zeros((HEAD, block), F32)
        for first, count, skip in key_parts(begin, block):
            expo = jnp.exp(held[first : first + count, skip:] - top[:, skip:])
            total += widen(jnp.sum(expo, axis=0, keepdims=True), skip, 0.0)
            part = dot(qkv_ref[2 * HEAD : 3 * HEAD, first : first + count], expo.astype(BF16))
            result += widen(part, skip, 0.0)
        out_ref[:, here] = (result / total).astype(BF16)
        lse_ref[0, 0:1, here] = top + jnp.log(total)


def attend(starts, qkv, first, heads, wait, through):
    rows = qkv.shape[1]
    return call(
        functools.partial(attend_kernel, len(through)),
        (heads,),
        [whole_spec(starts.shape), pl.BlockSpec((3 * HEAD, rows), lambda h: (h + first, 0))]
        + kept((*through, *wait)),
        [pl.BlockSpec((HEAD, rows), lambda h: (h, 0)), pl.BlockSpec((1, 1, rows), lambda h: (h, 0, 0))]
        + kept(through),
        [jax.ShapeDtypeStruct((heads * HEAD, rows), BF16), jax.ShapeDtypeStruct((heads, 1, rows), F32)]
        + [jax.ShapeDtypeStruct(item.shape, item.dtype) for item in through],
        [pltpu.VMEM((rows, HEAD), BF16), pltpu.VMEM((rows, min(BLOCK, rows)), F32)],
        "attend",
        work=heads * MICROSECOND,
        aliases={2 + index: 2 + index for index in range(len(through))},
    )(starts, qkv, *through, *wait)


def attend_back_kernel(start_ref, cos_ref, sin_ref, qkv_ref, grad_ref, out_ref, lse_ref, *refs):
    mixed_ref, keys, values, key_sum, value_sum = refs[-5:]
    rows = qkv_ref.shape[1]
    block = min(BLOCK, rows)
    keys[...] = qkv_ref[HEAD : 2 * HEAD, :].T
    values[...] = qkv_ref[2 * HEAD : 3 * HEAD, :].T
    key_sum[...] = jnp.zeros_like(key_sum)
    value_sum[...] = jnp.zeros_like(value_sum)

    def put_unrotated(base, here, grads):
        cosine, sine = cos_ref[:, here], sin_ref[:, here]
        one, two = grads[0:HALF, :], grads[HALF:ROT, :]
        turned = jnp.concatenate(
            [one * cosine + two * sine, two * cosine - one * sine, grads[ROT:, :]], axis=0
        )
        mixed_ref[base : base + HEAD, here] = turned.astype(BF16)

    for begin in range(0, rows, block):
        here = slice(begin, begin + block)
        queries, grads, starts = qkv_ref[0:HEAD, here], grad_ref[:, here], start_ref[0:1, here]
        lse = lse_ref[0, 0:1, here]
        inner = jnp.sum(grads.astype(F32) * out_ref[:, here].astype(F32), axis=0, keepdims=True)
        query_rows, grad_rows = queries.T, grads.T
        query_sum = jnp.zeros((HEAD, block), F32)
        for first, count, skip in key_parts(begin, block):
            there = slice(first, first + count)
            scores = masked(dot(keys[there, :], queries[:, skip:]), first, begin + skip, starts[:, skip:])
            probs = jnp.exp(scores - lse[:, skip:])
            score_grads = (probs * (dot(values[there, :], grads[:, skip:]) - inner[:, skip:])).astype(BF16)
            query_sum += widen(dot(qkv_ref[HEAD : 2 * HEAD, there], score_grads), skip, 0.0)
            key_sum[there, :] += dot(score_grads, query_rows[skip:, :])
            value_sum[there, :] += dot(probs.astype(BF16), grad_rows[skip:, :])
        put_unrotated(0, here, query_sum * SCALE)
    put_unrotated(HEAD, slice(0, rows), key_sum[...].T)
    mixed_ref[2 * HEAD : 3 * HEAD, :] = value_sum[...].T.astype(BF16)


def attend_back(starts, cosine, sine, qkv, grads, out, lse, first, wait):
    rows = qkv.shape[1]
    heads = lse.shape[0]
    return call(
        attend_back_kernel,
        (heads,),
        [
            whole_spec(starts.shape),
            whole_spec(cosine.shape),
            whole_spec(sine.shape),
            pl.BlockSpec((3 * HEAD, rows), lambda h: (h + first, 0)),
            pl.BlockSpec((HEAD, rows), lambda h: (h + first, 0)),
            pl.BlockSpec((HEAD, rows), lambda h: (h, 0)),
            pl.BlockSpec((1, 1, rows), lambda h: (h, 0, 0)),
            *kept(wait),
        ],
        pl.BlockSpec((3 * HEAD, rows), lambda h: (h, 0)),
        jax.ShapeDtypeStruct((heads * 3 * HEAD, rows), BF16),
        [pltpu.VMEM((rows, HEAD), BF16)] * 2 + [pltpu.VMEM((rows, HEAD), F32)] * 2,
        "attend_back",
        work=9 * heads * MICROSECOND,
    )(starts, cosine, sine, qkv, grads, out, lse, *wait)


def feed_kernel(place, order, *refs):
    dy_refs, refs = refs[:4], refs[4:]
    two_ref, weight_ref, att_refs, refs = refs[0], refs[1], refs[2:-21], refs[-21:]
    col_ref, *refs = refs
    branch_refs, (normed_ref, att_grad_ref, weights_ref, vector_ref), refs = refs[:4], refs[4:8], refs[8:]
    dy_now, up, down, dense, up_t, down_t, dense_t, active, hidden_grad, sums, vectors, held = refs
    step = pl.program_id(0)
    hidden_count = up.shape[1]
    dense_count = dense.shape[1]

    @pl.when(step == 0)
    def _():
        for here, there in blocks_of(order, up.shape[0]):
            up[here, :] = weight_ref[there, :hidden_count]
            down[here, :] = weight_ref[there, hidden_count : 2 * hidden_count]
            dense[here, :] = weight_ref[there, 2 * hidden_count :]
        up_t[...] = up[...].T
        down_t[...] = down[...].T
        dense_t[...] = dense[...].T
        sums[...] = jnp.zeros_like(sums)
        vectors[...] = jnp.zeros_like(vectors)

    dy = choose(dy_refs, step, dy_now)
    normed = two_ref[0]
    attended = jnp.concatenate([ref[...] for ref in att_refs], axis=0)
    att_grad_ref[...] = dot(dense_t[...], dy).astype(BF16)
    chunk = min(CHUNK, hidden_count)
    for first in range(0, hidden_count, chunk):
        units = slice(first, first + chunk)
        hidden = dot(up_t[units, :], normed) + col_ref[units, 4:5]
        chance = 0.5 + 0.5 * lax.erf(hidden * (0.5**0.5))
        density = jnp.exp(hidden * hidden * -0.5) * (hidden * 0.3989422804014327)
        now = (hidden * chance).astype(BF16)
        back = (dot(down_t[units, :], dy) * (chance + density)).astype(BF16)
        active[units, :] = now
        hidden_grad[units, :] = back
        sums[:, units] += dot_nt(normed, back)
        sums[:, hidden_count + first : hidden_count + first + chunk] += dot_nt(dy, now)
        vectors[3, units, :] += fold(back.astype(F32))
    sums[:, 2 * hidden_count :] += dot_nt(dy, attended)
    branch = (dot(dense[...], attended) + dot(down[...], active[...])).astype(BF16)
    for index, ref in enumerate(branch_refs):

        @pl.when(step == index)
        def _(ref=ref):
            ref[...] = branch

    normed_grad = dot(up[...], hidden_grad[...])
    normed_ref[0] = (normed_grad * column(col_ref, 2)).astype(BF16)
    vectors[0] += fold(normed_grad * normed.astype(F32))
    vectors[1] += fold(normed_grad)
    vectors[2] += fold(dy.astype(F32))

    @pl.when(step == pl.num_programs(0) - 1)
    def _():
        for here, there in blocks_of(order, sums.shape[0]):
            weights_ref[there, :] = sums[here, :].astype(BF16)
        gains = by_unit(vectors[0], vectors[1], col_ref, 2)
        rows = as_rows([gains, vectors[1], vectors[2]], order, held)
        vector_ref[...] = jnp.concatenate([rows[0:3], as_rows([vectors[3]])[0:5]], axis=0)


def feed(place, order, dy_all, normed, weights, attended, columns):
    width, slab = dy_all[0].shape
    parts = len(dy_all)
    dense_count = sum(item.shape[0] for item in attended)
    hidden_count = (weights.shape[1] - dense_count) // 2
    grad_cols = 2 * hidden_count + dense_count
    by_place = lambda s, t, _: (0, s ^ t[0])
    return call(
        feed_kernel,
        (parts,),
        [whole_spec(item.shape) for item in dy_all]
        + [pl.BlockSpec((1, width, slab), lambda s, *_: (s, 0, 0)), whole_spec(weights.shape)]
        + [pl.BlockSpec((item.shape[0], slab), by_place) for item in attended]
        + [whole_spec(columns.shape)],
        [whole_spec((width, slab))] * parts
        + [
            pl.BlockSpec((1, width, slab), lambda s, *_: (s, 0, 0)),
            pl.BlockSpec((dense_count, slab), by_place),
            whole_spec((width, grad_cols)),
            whole_spec((8, hidden_count)),
        ],
        [jax.ShapeDtypeStruct((width, slab), BF16)] * parts
        + [
            jax.ShapeDtypeStruct((parts, width, slab), BF16),
            jax.ShapeDtypeStruct((dense_count, parts * slab), BF16),
            jax.ShapeDtypeStruct((width, grad_cols), BF16),
            jax.ShapeDtypeStruct((8, hidden_count), F32),
        ],
        [
            pltpu.VMEM((width, slab), BF16),
            pltpu.VMEM((width, hidden_count), BF16),
            pltpu.VMEM((width, hidden_count), BF16),
            pltpu.VMEM((width, dense_count), BF16),
            pltpu.VMEM((hidden_count, width), BF16),
            pltpu.VMEM((hidden_count, width), BF16),
            pltpu.VMEM((dense_count, width), BF16),
            pltpu.VMEM((hidden_count, slab), BF16),
            pltpu.VMEM((hidden_count, slab), BF16),
            pltpu.VMEM((width, grad_cols), F32),
            pltpu.VMEM((4, hidden_count, 128), F32),
            pltpu.VMEM((width, 128), F32),
        ],
        "feed",
        prefetch=2,
        work=30 * MICROSECOND,
    )(place, order, *dy_all, normed, weights, *attended, columns)


def project_back_kernel(count, heads, place, order, *refs):
    one_ref, pieces, refs = refs[0], refs[1 : 1 + count], refs[1 + count :]
    mixed_refs, refs = refs[:heads], refs[heads:]
    part_ref, col_ref, refs = refs[0], refs[1], refs[-12:]
    unit_refs, (own_ref, sent_ref, vector_ref), refs = refs[:4], refs[4:7], refs[7:]
    w, sums, vectors, counts, held = refs
    step = pl.program_id(0)

    @pl.when(step == 0)
    def _():
        w[...] = join(pieces, 0, w.shape[1])
        sums[...] = jnp.zeros_like(sums)
        vectors[...] = jnp.zeros_like(vectors)
        counts[...] = jnp.zeros_like(counts)

    normed = one_ref[0]
    mixed = jnp.concatenate([ref[...] for ref in mixed_refs], axis=0)
    sums[...] += dot_nt(normed, mixed)
    counts[...] += fold(mixed.astype(F32))
    normed_grad = dot(w[...], mixed)
    total = (part_ref[0].astype(F32) + normed_grad * column(col_ref, 0)).astype(BF16)
    for index, ref in enumerate(unit_refs):

        @pl.when(step == index)
        def _(ref=ref):
            ref[...] = total

    vectors[0] += fold(normed_grad * normed.astype(F32))
    vectors[1] += fold(normed_grad)

    @pl.when(step == pl.num_programs(0) - 1)
    def _():
        half = own_ref.shape[0]
        own_ref[...] = sums[:half, :].astype(BF16)
        sent_ref[...] = sums[half:, :].astype(BF16)
        gains = by_unit(vectors[0], vectors[1], col_ref, 0)
        rows = as_rows([gains, vectors[1]], order, held)
        tail = as_rows([counts[...]])[0:6]
        tail = jnp.concatenate([tail, jnp.zeros((6, rows.shape[1] - tail.shape[1]), F32)], axis=1)
        vector_ref[...] = jnp.concatenate([rows[0:2], tail], axis=0)


def project_back(place, order, normed, pieces, mixed, part, columns, wait):
    parts, width, slab = normed.shape
    cols = sum(item.shape[0] for item in mixed)
    return call(
        functools.partial(project_back_kernel, len(pieces), len(mixed)),
        (parts,),
        [pl.BlockSpec((1, width, slab), lambda s, *_: (s, 0, 0))]
        + [whole_spec(item.shape) for item in pieces]
        + [pl.BlockSpec((item.shape[0], slab), lambda s, t, _: (0, s ^ t[0])) for item in mixed]
        + [pl.BlockSpec((1, width, slab), lambda s, *_: (s, 0, 0)), whole_spec(columns.shape)]
        + kept(wait),
        [whole_spec((width, slab))] * parts
        + [
            whole_spec((width // 2, cols)),
            whole_spec((width // 2, cols)),
            whole_spec((8, width)),
        ],
        [jax.ShapeDtypeStruct((width, slab), BF16)] * parts
        + [
            jax.ShapeDtypeStruct((width // 2, cols), BF16),
            jax.ShapeDtypeStruct((width // 2, cols), BF16),
            jax.ShapeDtypeStruct((8, width), F32),
        ],
        [
            pltpu.VMEM((width, cols), BF16),
            pltpu.VMEM((width, cols), F32),
            pltpu.VMEM((2, width, 128), F32),
            pltpu.VMEM((cols, 128), F32),
            pltpu.VMEM((width, 128), F32),
        ],
        "project_back",
        prefetch=2,
        work=13 * MICROSECOND,
    )(place, order, normed, *pieces, *mixed, part, columns, *wait)


def finish_out_kernel(order, own_ref, near_ref, far_ref, x_ref, bias_ref, *refs):
    out_ref, held = refs[-2:]
    branch = own_ref[...].astype(F32) + near_ref[...].astype(F32) + far_ref[...].astype(F32)
    out = (x_ref[...].astype(F32) + branch + column(bias_ref, 6)).astype(BF16)
    out_ref[...] = turn_back(order, held, out)


def finish_grad_kernel(order, own_ref, near_ref, far_ref, x_ref, dy_ref, *refs):
    out_ref, held = refs[-2:]
    grads = own_ref[...].astype(F32) + near_ref[...].astype(F32) + far_ref[...].astype(F32)
    values = x_ref[...].astype(F32)
    center = values - jnp.mean(values, axis=0, keepdims=True)
    scale = lax.rsqrt(jnp.mean(center * center, axis=0, keepdims=True) + EPS)
    unit = center * scale
    along = jnp.mean(grads * unit, axis=0, keepdims=True)
    level = jnp.mean(grads, axis=0, keepdims=True)
    out = dy_ref[...].astype(F32) + scale * (grads - level - unit * along)
    out_ref[...] = turn_back(order, held, out)


def finish(kernel, order, summands, own, other, kind, name, work, wait=()):
    width, count = own.shape
    part = min(256, count)
    block = pl.BlockSpec((width, part), lambda i, _: (0, i))
    return call(
        kernel,
        (count // part,),
        [block] * (len(summands) + 1)
        + [block if other.shape == own.shape else whole_spec(other.shape)]
        + kept(wait),
        pl.BlockSpec((part, width), lambda i, _: (i, 0)),
        jax.ShapeDtypeStruct((count, width), kind),
        [pltpu.VMEM((width, part), kind)],
        name,
        prefetch=1,
        work=work * MICROSECOND,
    )(order, *summands, own, other, *wait)


def share_kernel(own_ref, near_ref, *refs):
    refs[-1][...] = (own_ref[...].astype(F32) + near_ref[...].astype(F32)).astype(BF16)


def share(own, near, wait):
    width, count = own.shape
    block = pl.BlockSpec((width, count // 2), lambda i: (0, i))
    return call(
        share_kernel,
        (2,),
        [block, block] + kept(wait),
        block,
        jax.ShapeDtypeStruct(own.shape, BF16),
        [],
        "share",
    )(own, near, *wait)


def halve_kernel(own_ref, came_ref, *refs):
    outs = refs[-4:]
    size = outs[0].shape[0]
    for index, ref in enumerate(outs):
        rows = slice(index * size, (index + 1) * size)
        ref[...] = (own_ref[rows, :].astype(F32) + came_ref[rows, :].astype(F32)).astype(ref.dtype)


def halve(own, came, wait):
    shape = (own.shape[0] // 4, own.shape[1])
    return call(
        halve_kernel,
        (1,),
        [whole_spec(own.shape), whole_spec(came.shape), *kept(wait)],
        [whole_spec(shape)] * 4,
        [jax.ShapeDtypeStruct(shape, kind) for kind in (F32, BF16, BF16, BF16)],
        [],
        "halve",
    )(own, came, *wait)


def parts_kernel(whole_ref, *refs):
    at = 0
    for ref in refs[-3:]:
        ref[...] = whole_ref[:, at : at + ref.shape[1]].astype(F32)
        at += ref.shape[1]


def parts(whole, counts, wait):
    shapes = [(whole.shape[0], count) for count in counts]
    return call(
        parts_kernel,
        (1,),
        [whole_spec(whole.shape)] + kept(wait),
        [whole_spec(shape) for shape in shapes],
        [jax.ShapeDtypeStruct(shape, F32) for shape in shapes],
        [],
        "parts",
    )(whole, *wait)


def total_kernel(at, kept_ref, *refs):
    came, (kept_rows, *came_rows), refs = refs[:3], refs[3:7], refs[-9:]
    out_ref, norm_refs, dy_sum_ref, hidden_ref, qkv_ref = refs[0], refs[1:5], refs[5], refs[6], refs[7]
    out_ref[...] = kept_ref[...] + sum(ref[...].astype(F32) for ref in came)
    rows = kept_rows[...] + sum(ref[...] for ref in came_rows)
    width = rows.shape[1]
    norms = pltpu.roll(rows, width - at[0], 1)
    for index, ref in enumerate((*norm_refs, dy_sum_ref, refs[8])):
        row = min(index, 4)
        ref[...] = norms[row, 0 : ref.shape[0]]
    hidden_ref[...] = pltpu.roll(rows, width - at[1], 1)[5, 0 : hidden_ref.shape[0]]
    qkv_ref[...] = pltpu.roll(rows, width - at[2], 1)[6, 0 : qkv_ref.shape[0]]


def total(at, items, rows, counts, wait):
    norm, hidden, qkv = counts
    shapes = [items[0].shape] + [(norm,)] * 5 + [(hidden,), (qkv,), (norm,)]
    return call(
        total_kernel,
        (1,),
        [whole_spec(item.shape) for item in (*items, *rows)] + kept(wait),
        [whole_spec(shape) for shape in shapes],
        [jax.ShapeDtypeStruct(shape, F32) for shape in shapes],
        [],
        "total",
        prefetch=1,
    )(at, *items, *rows, *wait)


def gate_kernel(*refs):
    pass


def gate(items, wait):
    return call(
        gate_kernel,
        (1,),
        kept((*items, *wait)),
        kept(items),
        [jax.ShapeDtypeStruct(item.shape, item.dtype) for item in items],
        [],
        "gate",
        aliases={index: index for index in range(len(items))},
    )(*items, *wait)


def swap(value, axis, bits):
    count = lax.axis_size(axis)
    return lax.ppermute(value, axis, [(i, i ^ bits) for i in range(count)])


def gather_group(own):
    far = swap(own, "tensor", 2)
    near = swap(own, "tensor", 1)
    return (own, near, far, swap(far, "tensor", 1))


def scatter_group(slabs):
    far = (slabs[2].astype(F32) + swap(slabs[3], "tensor", 1).astype(F32)).astype(BF16)
    return (slabs[0], swap(slabs[1], "tensor", 1), swap(far, "tensor", 2)), (far,)


PARTNERS = (0, 2, 4, 6, 1, 3, 5, 7)


def paired():
    return lax.axis_size("dp") == len(PARTNERS)


def feature_order():
    if paired():
        return jnp.array(PARTNERS, jnp.int32) ^ lax.axis_index("dp").astype(jnp.int32)
    return jnp.zeros((1,), jnp.int32)


def gather_rows(own):
    if not paired():
        return (lax.all_gather(own, "dp", axis=0, tiled=True),)
    same = [own] + [swap(own, "dp", bits) for bits in PARTNERS[1:4]]
    return (*same, *(swap(piece, "dp", 1) for piece in same))


def partner_sums(own, sent):
    kept_block, *outward = halve(own, swap(sent, "dp", 1), ())
    return (kept_block, *(swap(half, "dp", bits) for half, bits in zip(outward, PARTNERS[1:4])))


def vector_sums(norms, others):
    rows = jnp.concatenate([norms, others], axis=0)
    rows = rows + swap(rows, "dp", 1)
    return (rows, *(swap(rows, "dp", bits) for bits in PARTNERS[1:4]))


def body(
    tokens,
    segment_ids,
    ln1_gain,
    ln1_bias,
    ln2_gain,
    ln2_bias,
    w_qkv,
    b_qkv,
    w_dense,
    b_dense,
    w_fc1,
    b_fc1,
    w_fc2,
    b_fc2,
    cotangent,
):
    group_rows = segment_ids.shape[0]
    width = tokens.shape[1]
    own_width = w_qkv.shape[0]
    dp_count = lax.axis_size("dp")
    tensor_count = lax.axis_size("tensor")
    mine = lax.axis_index("tensor").astype(jnp.int32)
    place = mine.reshape(1)
    order = feature_order()

    firsts = gather_rows(w_qkv)
    x_all = gather_group(turn(order, tokens))
    weights = lax.all_gather(jnp.concatenate([w_fc1, w_fc2, w_dense], axis=1), "dp", axis=0, tiled=True)
    rows = jnp.stack([ln1_gain, ln1_bias, ln2_gain, ln2_bias, b_fc1, jnp.pad(b_qkv, (0, width - b_qkv.shape[0])), b_dense + b_fc2])
    columns = stand(order, jnp.pad(rows, ((0, 1), (0, 0))), ())
    (dy_own,) = gate([turn(order, cotangent)], (x_all[2], *firsts[4:]))
    dy_far, dy_near = swap(dy_own, "tensor", 2), swap(dy_own, "tensor", 1)

    row = jnp.arange(group_rows, dtype=jnp.int32)
    padding = segment_ids != segment_ids[0]
    length = jnp.sum(jnp.where(padding, 0, 1))
    starts = jnp.where(padding, length, 0)
    inverse = 10000.0 ** (-jnp.arange(0, ROT, 2, dtype=F32) / ROT)
    angles = inverse[:, None] * (row - starts).astype(F32)[None, :]
    cosine, sine = jnp.cos(angles), jnp.sin(angles)
    starts = starts[None, :]

    qkv, normed_one, normed_two = project(place, x_all, firsts, columns, cosine, sine, (dy_own,))
    heads = range(qkv.shape[0] // (3 * HEAD))
    attended, lse = [], []
    for head in heads:
        through = (dy_far,) if head == 1 else ()
        result, scale, *through = attend(starts, qkv, head, 1, attended[-1:], through)
        attended.append(result)
        lse.append(scale)
        if head == 1:
            (dy_far,) = through
    dy_all = (dy_own, dy_near, dy_far, swap(dy_far, "tensor", 1))
    *branch, part, att_grad, feed_grads, feed_vectors = feed(
        place, order, dy_all, normed_two, weights, attended, columns
    )
    feed_grads = lax.psum_scatter(feed_grads, "dp", scatter_dimension=0, tiled=True)
    counts = (w_fc1.shape[1], w_fc2.shape[1], w_dense.shape[1])
    out_summands, branch_wait = scatter_group(branch)

    mixed_grad = []
    for head in heads:
        wait = (*branch_wait, *mixed_grad[-1:]) if head == 1 else mixed_grad[-1:]
        mixed_grad.append(
            attend_back(starts, cosine, sine, qkv, att_grad, attended[head], lse[head], head, wait)
        )
    *unit_grad, qkv_own, qkv_sent, last_vectors = project_back(
        place, order, normed_one, firsts, mixed_grad, part, columns, out_summands[2:]
    )
    norms = jnp.concatenate([last_vectors[0:2], feed_vectors[0:2]], axis=0)
    others = jnp.concatenate([feed_vectors[2:4], last_vectors[2:4]], axis=0)
    if paired():
        norms = norms + swap(norms, "tensor", 1) + swap(norms, "tensor", 2) + swap(norms, "tensor", 3)
    else:
        norms = lax.psum(norms, "tensor")
    far = share(unit_grad[2], swap(unit_grad[3], "tensor", 1), (norms,))
    summands = (unit_grad[0], swap(unit_grad[1], "tensor", 1), swap(far, "tensor", 2))
    input_grad = finish(
        finish_grad_kernel, order, summands, x_all[0], dy_own, F32, "finish_grad", 0
    )
    out = finish(
        finish_out_kernel, order, out_summands, x_all[0], columns, BF16, "finish_out", 0, (far,)
    )
    norm_count, bias_count = own_width // tensor_count, b_qkv.shape[0] // dp_count
    at = lax.axis_index("dp").astype(jnp.int32) * jnp.array([own_width, own_width, bias_count], jnp.int32)
    at = at + mine * jnp.array([norm_count, 0, 0], jnp.int32)
    up_grad, down_grad, dense_grad = parts(feed_grads, counts, (input_grad,))
    if paired():
        qkv_grads, *vectors = total(
            at,
            partner_sums(qkv_own, qkv_sent),
            vector_sums(norms, others),
            (norm_count, own_width, bias_count),
            (input_grad,),
        )
    else:
        qkv_grads = jnp.concatenate([qkv_own, qkv_sent], axis=0)
        qkv_grads = lax.psum_scatter(qkv_grads, "dp", scatter_dimension=0, tiled=True).astype(F32)
        rows = lax.psum(jnp.concatenate([norms, others], axis=0), "dp")
        vectors = [lax.dynamic_slice_in_dim(rows[index], at[0], norm_count, 0) for index in range(5)]
        vectors += [lax.dynamic_slice_in_dim(rows[5], at[1], own_width, 0)]
        vectors += [lax.dynamic_slice_in_dim(rows[6], at[2], bias_count, 0), vectors[4]]
    return (
        out,
        input_grad,
        *vectors[:4],
        qkv_grads,
        vectors[6],
        dense_grad,
        vectors[4],
        up_grad,
        vectors[5],
        down_grad,
        vectors[7],
    )


def solution(mesh):
    placed = (
        P(("dp", "tensor"), None),
        P("dp"),
        P(),
        P(),
        P(),
        P(),
        P("dp", "tensor"),
        P("tensor"),
        P("dp", "tensor"),
        P(),
        P("dp", "tensor"),
        P("tensor"),
        P("dp", "tensor"),
        P(),
        P(("dp", "tensor"), None),
    )
    return jax.shard_map(
        body,
        mesh=mesh,
        in_specs=placed,
        out_specs=(
            P(("dp", "tensor"), None),
            P(("dp", "tensor"), None),
            P(("dp", "tensor")),
            P(("dp", "tensor")),
            P(("dp", "tensor")),
            P(("dp", "tensor")),
            P("dp", "tensor"),
            P(("tensor", "dp")),
            P("dp", "tensor"),
            P(("dp", "tensor")),
            P("dp", "tensor"),
            P(("tensor", "dp")),
            P("dp", "tensor"),
            P(("dp", "tensor")),
        ),
        check_vma=False,
    )
```

```python
import functools

import jax
import jax.numpy as jnp
from jax import lax
from jax.experimental import pallas as pl
from jax.experimental.pallas import tpu as pltpu
from jax.sharding import PartitionSpec as P

HEAD = 64
ROT = 16
HALF = ROT // 2
EPS = 1e-05
NEG = -1e30
SCALE = HEAD ** (-0.5)
WHOLE = 1536
BLOCK = 512
F32 = jnp.float32
BF16 = jnp.bfloat16
VMEM_LIMIT = 56 * 1024 * 1024
MICROSECOND = 1_150_000_000
CHUNK = 768


def dot(left, right):
    return jnp.dot(left, right, preferred_element_type=F32)


def dot_nt(left, right):
    return lax.dot_general(left, right, (((1,), (1,)), ((), ())), preferred_element_type=F32)


def call(kernel, grid, in_specs, out_specs, out_shape, scratch, name, prefetch=0, work=0, aliases={}):
    return pl.pallas_call(
        kernel,
        grid_spec=pltpu.PrefetchScalarGridSpec(
            num_scalar_prefetch=prefetch,
            grid=grid,
            in_specs=in_specs,
            out_specs=out_specs,
            scratch_shapes=scratch,
        ),
        out_shape=out_shape,
        compiler_params=pltpu.CompilerParams(vmem_limit_bytes=VMEM_LIMIT),
        cost_estimate=pl.CostEstimate(flops=work, bytes_accessed=0, transcendentals=0),
        input_output_aliases=aliases,
        name=name,
    )


def whole_spec(shape):
    return pl.BlockSpec(shape, lambda *_: (0,) * len(shape))


def column(ref, index):
    return ref[:, index : index + 1]


def join(pieces, first, count):
    return jnp.concatenate([piece[:, first : first + count] for piece in pieces], axis=0)


def blocks_of(order, rows):
    count = order.shape[0]
    size = rows // count
    return [
        (slice(at * size, (at + 1) * size), pl.ds(pl.multiple_of(order[at] * size, size), size))
        for at in range(count)
    ]


def choose(refs, step, held):
    for index, ref in enumerate(refs):

        @pl.when(step == index)
        def _(ref=ref):
            held[...] = ref[...]

    return held[...]


def fold(values):
    return sum(values[:, at : at + 128] for at in range(0, values.shape[1], 128))


def as_rows(parts, order=None, held=None):
    sums = [jnp.sum(part, axis=1, keepdims=True) for part in parts]
    lane = lax.broadcasted_iota(jnp.int32, parts[0].shape, 1)
    total = jnp.zeros(parts[0].shape, F32)
    for index, item in enumerate(sums):
        total = jnp.where(lane == index, item, total)
    if order is None:
        return total.T[0:8, :]
    return turn_back(order, held, total)[0:8, :]


def by_unit(along, level, col_ref, index):
    return (along - level * column(col_ref, index + 1)) / column(col_ref, index)


def kept(items):
    return [pl.BlockSpec(memory_space=pl.ANY) for _ in items]


def standardize(block):
    values = block.astype(F32)
    center = values - jnp.mean(values, axis=0, keepdims=True)
    spread = jnp.mean(center * center, axis=0, keepdims=True)
    return center * lax.rsqrt(spread + EPS)


def turn_kernel(order, rows_ref, *refs):
    out_ref, held = refs[-2:]
    held[...] = rows_ref[...].T
    for here, there in blocks_of(order, out_ref.shape[0]):
        out_ref[here, :] = held[there, :]


def turn(order, rows, wait=()):
    count, width = rows.shape
    part = min(256, count)
    return call(
        turn_kernel,
        (count // part,),
        [pl.BlockSpec((part, width), lambda i, _: (i, 0)), *kept(wait)],
        pl.BlockSpec((width, part), lambda i, _: (0, i)),
        jax.ShapeDtypeStruct((width, count), rows.dtype),
        [pltpu.VMEM((width, part), rows.dtype)],
        "turn",
        prefetch=1,
    )(order, rows, *wait)


def turn_back(order, held, grads):
    for here, there in blocks_of(order, grads.shape[0]):
        held[there, :] = grads[here, :]
    return held[...].T


def stand_kernel(order, rows_ref, *refs):
    out_ref, held = refs[-2:]
    rows = rows_ref[...]
    held[...] = jnp.concatenate([rows, jnp.zeros((128 - rows.shape[0], rows.shape[1]), F32)], axis=0).T
    count = order.shape[0]
    size = rows.shape[1] // count
    lane = lax.broadcasted_iota(jnp.int32, (size, 128), 1)
    for index in range(count):
        first = pl.multiple_of(order[index] * size, size)
        here = slice(index * size, (index + 1) * size)
        out_ref[here, :] = jnp.where((lane < 4) | (lane == 6), held[pl.ds(first, size), :], held[here, :])


def stand(order, rows, wait):
    shape = (rows.shape[1], 128)
    return call(
        stand_kernel,
        (1,),
        [whole_spec(rows.shape), *kept(wait)],
        whole_spec(shape),
        jax.ShapeDtypeStruct(shape, F32),
        [pltpu.VMEM(shape, F32)],
        "stand",
        prefetch=1,
    )(order, rows, *wait)


def project_kernel(count, place, *refs):
    x_refs, pieces, refs = refs[:4], refs[4 : 4 + count], refs[4 + count :]
    col_ref, cos_ref, sin_ref = refs[:3]
    out_ref, one_ref, two_ref, x_now, wt = refs[-5:]
    step = pl.program_id(0)
    cols = out_ref.shape[0]

    @pl.when(step == 0)
    def _():
        wt[...] = join(pieces, 0, cols).T

    unit = standardize(choose(x_refs, step, x_now))
    normed = (unit * column(col_ref, 0) + column(col_ref, 1)).astype(BF16)
    one_ref[0] = normed
    two_ref[0] = (unit * column(col_ref, 2) + column(col_ref, 3)).astype(BF16)
    cosine, sine = cos_ref[...], sin_ref[...]
    joined = dot(wt[...], normed) + col_ref[:cols, 5:6]
    for head in range(cols // (3 * HEAD)):
        base = head * 3 * HEAD
        mixed = joined[base : base + 3 * HEAD, :]
        for part, factor in ((0, SCALE), (HEAD, 1.0)):
            one, two = mixed[part : part + HALF], mixed[part + HALF : part + ROT]
            turned = jnp.concatenate(
                [one * cosine - two * sine, two * cosine + one * sine, mixed[part + ROT : part + HEAD]],
                axis=0,
            )
            out_ref[base + part : base + part + HEAD, :] = (turned * factor).astype(BF16)
        out_ref[base + 2 * HEAD : base + 3 * HEAD, :] = mixed[2 * HEAD :].astype(BF16)


def project(place, x_all, pieces, columns, cosine, sine, wait):
    width, slab = x_all[0].shape
    cols = pieces[0].shape[1]
    by_place = lambda s, t: (0, s ^ t[0])
    return call(
        functools.partial(project_kernel, len(pieces)),
        (len(x_all),),
        [whole_spec(item.shape) for item in (*x_all, *pieces, columns)]
        + [pl.BlockSpec((HALF, slab), by_place), pl.BlockSpec((HALF, slab), by_place), *kept(wait)],
        [
            pl.BlockSpec((cols, slab), by_place),
            pl.BlockSpec((1, width, slab), lambda s, t: (s, 0, 0)),
            pl.BlockSpec((1, width, slab), lambda s, t: (s, 0, 0)),
        ],
        [
            jax.ShapeDtypeStruct((cols, len(x_all) * slab), BF16),
            jax.ShapeDtypeStruct((len(x_all), width, slab), BF16),
            jax.ShapeDtypeStruct((len(x_all), width, slab), BF16),
        ],
        [pltpu.VMEM((width, slab), BF16), pltpu.VMEM((cols, width), BF16)],
        "project",
        prefetch=1,
        work=1 * MICROSECOND,
    )(place, *x_all, *pieces, columns, cosine, sine, *wait)


def masked(scores, first_key, first_query, starts):
    diagonal = first_key + scores.shape[0] > first_query
    ragged = first_query + scores.shape[1] > WHOLE
    if not (diagonal or ragged):
        return scores
    key = first_key + lax.broadcasted_iota(jnp.int32, scores.shape, 0)
    allowed = key >= starts
    if diagonal:
        allowed &= key <= first_query + lax.broadcasted_iota(jnp.int32, scores.shape, 1)
    return jnp.where(allowed, scores, NEG)


def key_parts(begin, block):
    half = block // 2
    parts = [(first, block, 0) for first in range(0, begin, block)]
    return parts + [(begin, half, 0), (begin + half, half, half)]


def widen(values, skip, fill):
    if not skip:
        return values
    return jnp.concatenate([jnp.full((values.shape[0], skip), fill, values.dtype), values], axis=1)


def attend_kernel(handed, start_ref, qkv_ref, *refs):
    out_ref, lse_ref = refs[-4 - handed : len(refs) - 2 - handed]
    keys, held = refs[-2:]
    rows = qkv_ref.shape[1]
    block = min(BLOCK, rows)
    keys[...] = qkv_ref[HEAD : 2 * HEAD, :].T
    for begin in range(0, rows, block):
        here = slice(begin, begin + block)
        queries, starts = qkv_ref[0:HEAD, here], start_ref[0:1, here]
        top = jnp.full((1, block), NEG, F32)
        for first, count, skip in key_parts(begin, block):
            scores = masked(dot(keys[first : first + count, :], queries[:, skip:]), first, begin + skip, starts[:, skip:])
            held[first : first + count, skip:] = scores
            top = jnp.maximum(top, widen(jnp.max(scores, axis=0, keepdims=True), skip, NEG))
        total = jnp.zeros((1, block), F32)
        result = jnp.zeros((HEAD, block), F32)
        for first, count, skip in key_parts(begin, block):
            expo = jnp.exp(held[first : first + count, skip:] - top[:, skip:])
            total += widen(jnp.sum(expo, axis=0, keepdims=True), skip, 0.0)
            part = dot(qkv_ref[2 * HEAD : 3 * HEAD, first : first + count], expo.astype(BF16))
            result += widen(part, skip, 0.0)
        out_ref[:, here] = (result / total).astype(BF16)
        lse_ref[0, 0:1, here] = top + jnp.log(total)


def attend(starts, qkv, first, heads, wait, through):
    rows = qkv.shape[1]
    return call(
        functools.partial(attend_kernel, len(through)),
        (heads,),
        [whole_spec(starts.shape), pl.BlockSpec((3 * HEAD, rows), lambda h: (h + first, 0))]
        + kept((*through, *wait)),
        [pl.BlockSpec((HEAD, rows), lambda h: (h, 0)), pl.BlockSpec((1, 1, rows), lambda h: (h, 0, 0))]
        + kept(through),
        [jax.ShapeDtypeStruct((heads * HEAD, rows), BF16), jax.ShapeDtypeStruct((heads, 1, rows), F32)]
        + [jax.ShapeDtypeStruct(item.shape, item.dtype) for item in through],
        [pltpu.VMEM((rows, HEAD), BF16), pltpu.VMEM((rows, min(BLOCK, rows)), F32)],
        "attend",
        work=heads * MICROSECOND,
        aliases={2 + index: 2 + index for index in range(len(through))},
    )(starts, qkv, *through, *wait)


def attend_back_kernel(start_ref, cos_ref, sin_ref, qkv_ref, grad_ref, out_ref, lse_ref, *refs):
    mixed_ref, keys, values, key_sum, value_sum = refs[-5:]
    rows = qkv_ref.shape[1]
    block = min(BLOCK, rows)
    keys[...] = qkv_ref[HEAD : 2 * HEAD, :].T
    values[...] = qkv_ref[2 * HEAD : 3 * HEAD, :].T
    key_sum[...] = jnp.zeros_like(key_sum)
    value_sum[...] = jnp.zeros_like(value_sum)

    def put_unrotated(base, here, grads):
        cosine, sine = cos_ref[:, here], sin_ref[:, here]
        one, two = grads[0:HALF, :], grads[HALF:ROT, :]
        turned = jnp.concatenate(
            [one * cosine + two * sine, two * cosine - one * sine, grads[ROT:, :]], axis=0
        )
        mixed_ref[base : base + HEAD, here] = turned.astype(BF16)

    for begin in range(0, rows, block):
        here = slice(begin, begin + block)
        queries, grads, starts = qkv_ref[0:HEAD, here], grad_ref[:, here], start_ref[0:1, here]
        lse = lse_ref[0, 0:1, here]
        inner = jnp.sum(grads.astype(F32) * out_ref[:, here].astype(F32), axis=0, keepdims=True)
        query_rows, grad_rows = queries.T, grads.T
        query_sum = jnp.zeros((HEAD, block), F32)
        for first, count, skip in key_parts(begin, block):
            there = slice(first, first + count)
            scores = masked(dot(keys[there, :], queries[:, skip:]), first, begin + skip, starts[:, skip:])
            probs = jnp.exp(scores - lse[:, skip:])
            score_grads = (probs * (dot(values[there, :], grads[:, skip:]) - inner[:, skip:])).astype(BF16)
            query_sum += widen(dot(qkv_ref[HEAD : 2 * HEAD, there], score_grads), skip, 0.0)
            key_sum[there, :] += dot(score_grads, query_rows[skip:, :])
            value_sum[there, :] += dot(probs.astype(BF16), grad_rows[skip:, :])
        put_unrotated(0, here, query_sum * SCALE)
    put_unrotated(HEAD, slice(0, rows), key_sum[...].T)
    mixed_ref[2 * HEAD : 3 * HEAD, :] = value_sum[...].T.astype(BF16)


def attend_back(starts, cosine, sine, qkv, grads, out, lse, first, wait):
    rows = qkv.shape[1]
    heads = lse.shape[0]
    return call(
        attend_back_kernel,
        (heads,),
        [
            whole_spec(starts.shape),
            whole_spec(cosine.shape),
            whole_spec(sine.shape),
            pl.BlockSpec((3 * HEAD, rows), lambda h: (h + first, 0)),
            pl.BlockSpec((HEAD, rows), lambda h: (h + first, 0)),
            pl.BlockSpec((HEAD, rows), lambda h: (h, 0)),
            pl.BlockSpec((1, 1, rows), lambda h: (h, 0, 0)),
            *kept(wait),
        ],
        pl.BlockSpec((3 * HEAD, rows), lambda h: (h, 0)),
        jax.ShapeDtypeStruct((heads * 3 * HEAD, rows), BF16),
        [pltpu.VMEM((rows, HEAD), BF16)] * 2 + [pltpu.VMEM((rows, HEAD), F32)] * 2,
        "attend_back",
        work=9 * heads * MICROSECOND,
    )(starts, cosine, sine, qkv, grads, out, lse, *wait)


def feed_kernel(place, order, *refs):
    dy_refs, refs = refs[:4], refs[4:]
    two_ref, weight_ref, att_refs, refs = refs[0], refs[1], refs[2:-21], refs[-21:]
    col_ref, *refs = refs
    branch_refs, (normed_ref, att_grad_ref, weights_ref, vector_ref), refs = refs[:4], refs[4:8], refs[8:]
    dy_now, up, down, dense, up_t, down_t, dense_t, active, hidden_grad, sums, vectors, held = refs
    step = pl.program_id(0)
    hidden_count = up.shape[1]
    dense_count = dense.shape[1]

    @pl.when(step == 0)
    def _():
        for here, there in blocks_of(order, up.shape[0]):
            up[here, :] = weight_ref[there, :hidden_count]
            down[here, :] = weight_ref[there, hidden_count : 2 * hidden_count]
            dense[here, :] = weight_ref[there, 2 * hidden_count :]
        up_t[...] = up[...].T
        down_t[...] = down[...].T
        dense_t[...] = dense[...].T
        sums[...] = jnp.zeros_like(sums)
        vectors[...] = jnp.zeros_like(vectors)

    dy = choose(dy_refs, step, dy_now)
    normed = two_ref[0]
    attended = jnp.concatenate([ref[...] for ref in att_refs], axis=0)
    att_grad_ref[...] = dot(dense_t[...], dy).astype(BF16)
    chunk = min(CHUNK, hidden_count)
    for first in range(0, hidden_count, chunk):
        units = slice(first, first + chunk)
        hidden = dot(up_t[units, :], normed) + col_ref[units, 4:5]
        chance = 0.5 + 0.5 * lax.erf(hidden * (0.5**0.5))
        density = jnp.exp(hidden * hidden * -0.5) * (hidden * 0.3989422804014327)
        now = (hidden * chance).astype(BF16)
        back = (dot(down_t[units, :], dy) * (chance + density)).astype(BF16)
        active[units, :] = now
        hidden_grad[units, :] = back
        sums[:, units] += dot_nt(normed, back)
        sums[:, hidden_count + first : hidden_count + first + chunk] += dot_nt(dy, now)
        vectors[3, units, :] += fold(back.astype(F32))
    sums[:, 2 * hidden_count :] += dot_nt(dy, attended)
    branch = (dot(dense[...], attended) + dot(down[...], active[...])).astype(BF16)
    for index, ref in enumerate(branch_refs):

        @pl.when(step == index)
        def _(ref=ref):
            ref[...] = branch

    normed_grad = dot(up[...], hidden_grad[...])
    normed_ref[0] = (normed_grad * column(col_ref, 2)).astype(BF16)
    vectors[0] += fold(normed_grad * normed.astype(F32))
    vectors[1] += fold(normed_grad)
    vectors[2] += fold(dy.astype(F32))

    @pl.when(step == pl.num_programs(0) - 1)
    def _():
        for here, there in blocks_of(order, sums.shape[0]):
            weights_ref[there, :] = sums[here, :].astype(BF16)
        gains = by_unit(vectors[0], vectors[1], col_ref, 2)
        rows = as_rows([gains, vectors[1], vectors[2]], order, held)
        vector_ref[...] = jnp.concatenate([rows[0:3], as_rows([vectors[3]])[0:5]], axis=0)


def feed(place, order, dy_all, normed, weights, attended, columns):
    width, slab = dy_all[0].shape
    parts = len(dy_all)
    dense_count = sum(item.shape[0] for item in attended)
    hidden_count = (weights.shape[1] - dense_count) // 2
    grad_cols = 2 * hidden_count + dense_count
    by_place = lambda s, t, _: (0, s ^ t[0])
    return call(
        feed_kernel,
        (parts,),
        [whole_spec(item.shape) for item in dy_all]
        + [pl.BlockSpec((1, width, slab), lambda s, *_: (s, 0, 0)), whole_spec(weights.shape)]
        + [pl.BlockSpec((item.shape[0], slab), by_place) for item in attended]
        + [whole_spec(columns.shape)],
        [whole_spec((width, slab))] * parts
        + [
            pl.BlockSpec((1, width, slab), lambda s, *_: (s, 0, 0)),
            pl.BlockSpec((dense_count, slab), by_place),
            whole_spec((width, grad_cols)),
            whole_spec((8, hidden_count)),
        ],
        [jax.ShapeDtypeStruct((width, slab), BF16)] * parts
        + [
            jax.ShapeDtypeStruct((parts, width, slab), BF16),
            jax.ShapeDtypeStruct((dense_count, parts * slab), BF16),
            jax.ShapeDtypeStruct((width, grad_cols), BF16),
            jax.ShapeDtypeStruct((8, hidden_count), F32),
        ],
        [
            pltpu.VMEM((width, slab), BF16),
            pltpu.VMEM((width, hidden_count), BF16),
            pltpu.VMEM((width, hidden_count), BF16),
            pltpu.VMEM((width, dense_count), BF16),
            pltpu.VMEM((hidden_count, width), BF16),
            pltpu.VMEM((hidden_count, width), BF16),
            pltpu.VMEM((dense_count, width), BF16),
            pltpu.VMEM((hidden_count, slab), BF16),
            pltpu.VMEM((hidden_count, slab), BF16),
            pltpu.VMEM((width, grad_cols), F32),
            pltpu.VMEM((4, hidden_count, 128), F32),
            pltpu.VMEM((width, 128), F32),
        ],
        "feed",
        prefetch=2,
        work=30 * MICROSECOND,
    )(place, order, *dy_all, normed, weights, *attended, columns)


def project_back_kernel(count, heads, place, order, *refs):
    one_ref, pieces, refs = refs[0], refs[1 : 1 + count], refs[1 + count :]
    mixed_refs, refs = refs[:heads], refs[heads:]
    part_ref, col_ref, refs = refs[0], refs[1], refs[-12:]
    unit_refs, (own_ref, sent_ref, vector_ref), refs = refs[:4], refs[4:7], refs[7:]
    w, sums, vectors, counts, held = refs
    step = pl.program_id(0)

    @pl.when(step == 0)
    def _():
        w[...] = join(pieces, 0, w.shape[1])
        sums[...] = jnp.zeros_like(sums)
        vectors[...] = jnp.zeros_like(vectors)
        counts[...] = jnp.zeros_like(counts)

    normed = one_ref[0]
    mixed = jnp.concatenate([ref[...] for ref in mixed_refs], axis=0)
    sums[...] += dot_nt(normed, mixed)
    counts[...] += fold(mixed.astype(F32))
    normed_grad = dot(w[...], mixed)
    total = (part_ref[0].astype(F32) + normed_grad * column(col_ref, 0)).astype(BF16)
    for index, ref in enumerate(unit_refs):

        @pl.when(step == index)
        def _(ref=ref):
            ref[...] = total

    vectors[0] += fold(normed_grad * normed.astype(F32))
    vectors[1] += fold(normed_grad)

    @pl.when(step == pl.num_programs(0) - 1)
    def _():
        half = own_ref.shape[0]
        own_ref[...] = sums[:half, :].astype(BF16)
        sent_ref[...] = sums[half:, :].astype(BF16)
        gains = by_unit(vectors[0], vectors[1], col_ref, 0)
        rows = as_rows([gains, vectors[1]], order, held)
        tail = as_rows([counts[...]])[0:6]
        tail = jnp.concatenate([tail, jnp.zeros((6, rows.shape[1] - tail.shape[1]), F32)], axis=1)
        vector_ref[...] = jnp.concatenate([rows[0:2], tail], axis=0)


def project_back(place, order, normed, pieces, mixed, part, columns, wait):
    parts, width, slab = normed.shape
    cols = sum(item.shape[0] for item in mixed)
    return call(
        functools.partial(project_back_kernel, len(pieces), len(mixed)),
        (parts,),
        [pl.BlockSpec((1, width, slab), lambda s, *_: (s, 0, 0))]
        + [whole_spec(item.shape) for item in pieces]
        + [pl.BlockSpec((item.shape[0], slab), lambda s, t, _: (0, s ^ t[0])) for item in mixed]
        + [pl.BlockSpec((1, width, slab), lambda s, *_: (s, 0, 0)), whole_spec(columns.shape)]
        + kept(wait),
        [whole_spec((width, slab))] * parts
        + [
            whole_spec((width // 2, cols)),
            whole_spec((width // 2, cols)),
            whole_spec((8, width)),
        ],
        [jax.ShapeDtypeStruct((width, slab), BF16)] * parts
        + [
            jax.ShapeDtypeStruct((width // 2, cols), BF16),
            jax.ShapeDtypeStruct((width // 2, cols), BF16),
            jax.ShapeDtypeStruct((8, width), F32),
        ],
        [
            pltpu.VMEM((width, cols), BF16),
            pltpu.VMEM((width, cols), F32),
            pltpu.VMEM((2, width, 128), F32),
            pltpu.VMEM((cols, 128), F32),
            pltpu.VMEM((width, 128), F32),
        ],
        "project_back",
        prefetch=2,
        work=13 * MICROSECOND,
    )(place, order, normed, *pieces, *mixed, part, columns, *wait)


def finish_out_kernel(order, own_ref, near_ref, far_ref, x_ref, bias_ref, *refs):
    out_ref, held = refs[-2:]
    branch = own_ref[...].astype(F32) + near_ref[...].astype(F32) + far_ref[...].astype(F32)
    out = (x_ref[...].astype(F32) + branch + column(bias_ref, 6)).astype(BF16)
    out_ref[...] = turn_back(order, held, out)


def finish_grad_kernel(order, own_ref, near_ref, far_ref, x_ref, dy_ref, *refs):
    out_ref, held = refs[-2:]
    grads = own_ref[...].astype(F32) + near_ref[...].astype(F32) + far_ref[...].astype(F32)
    values = x_ref[...].astype(F32)
    center = values - jnp.mean(values, axis=0, keepdims=True)
    scale = lax.rsqrt(jnp.mean(center * center, axis=0, keepdims=True) + EPS)
    unit = center * scale
    along = jnp.mean(grads * unit, axis=0, keepdims=True)
    level = jnp.mean(grads, axis=0, keepdims=True)
    out = dy_ref[...].astype(F32) + scale * (grads - level - unit * along)
    out_ref[...] = turn_back(order, held, out)


def finish(kernel, order, summands, own, other, kind, name, work, wait=()):
    width, count = own.shape
    part = min(256, count)
    block = pl.BlockSpec((width, part), lambda i, _: (0, i))
    return call(
        kernel,
        (count // part,),
        [block] * (len(summands) + 1)
        + [block if other.shape == own.shape else whole_spec(other.shape)]
        + kept(wait),
        pl.BlockSpec((part, width), lambda i, _: (i, 0)),
        jax.ShapeDtypeStruct((count, width), kind),
        [pltpu.VMEM((width, part), kind)],
        name,
        prefetch=1,
        work=work * MICROSECOND,
    )(order, *summands, own, other, *wait)


def share_kernel(own_ref, near_ref, *refs):
    refs[-1][...] = (own_ref[...].astype(F32) + near_ref[...].astype(F32)).astype(BF16)


def share(own, near, wait):
    width, count = own.shape
    block = pl.BlockSpec((width, count // 2), lambda i: (0, i))
    return call(
        share_kernel,
        (2,),
        [block, block] + kept(wait),
        block,
        jax.ShapeDtypeStruct(own.shape, BF16),
        [],
        "share",
    )(own, near, *wait)


def halve_kernel(own_ref, came_ref, *refs):
    outs = refs[-4:]
    size = outs[0].shape[0]
    for index, ref in enumerate(outs):
        rows = slice(index * size, (index + 1) * size)
        ref[...] = (own_ref[rows, :].astype(F32) + came_ref[rows, :].astype(F32)).astype(ref.dtype)


def halve(own, came, wait):
    shape = (own.shape[0] // 4, own.shape[1])
    return call(
        halve_kernel,
        (1,),
        [whole_spec(own.shape), whole_spec(came.shape), *kept(wait)],
        [whole_spec(shape)] * 4,
        [jax.ShapeDtypeStruct(shape, kind) for kind in (F32, BF16, BF16, BF16)],
        [],
        "halve",
    )(own, came, *wait)


def parts_kernel(whole_ref, *refs):
    at = 0
    for ref in refs[-3:]:
        ref[...] = whole_ref[:, at : at + ref.shape[1]].astype(F32)
        at += ref.shape[1]


def parts(whole, counts, wait):
    shapes = [(whole.shape[0], count) for count in counts]
    return call(
        parts_kernel,
        (1,),
        [whole_spec(whole.shape)] + kept(wait),
        [whole_spec(shape) for shape in shapes],
        [jax.ShapeDtypeStruct(shape, F32) for shape in shapes],
        [],
        "parts",
    )(whole, *wait)


def total_kernel(at, kept_ref, *refs):
    came, (kept_rows, *came_rows), refs = refs[:3], refs[3:7], refs[-9:]
    out_ref, norm_refs, dy_sum_ref, hidden_ref, qkv_ref = refs[0], refs[1:5], refs[5], refs[6], refs[7]
    out_ref[...] = kept_ref[...] + sum(ref[...].astype(F32) for ref in came)
    rows = kept_rows[...] + sum(ref[...] for ref in came_rows)
    width = rows.shape[1]
    norms = pltpu.roll(rows, width - at[0], 1)
    for index, ref in enumerate((*norm_refs, dy_sum_ref, refs[8])):
        row = min(index, 4)
        ref[...] = norms[row, 0 : ref.shape[0]]
    hidden_ref[...] = pltpu.roll(rows, width - at[1], 1)[5, 0 : hidden_ref.shape[0]]
    qkv_ref[...] = pltpu.roll(rows, width - at[2], 1)[6, 0 : qkv_ref.shape[0]]


def total(at, items, rows, counts, wait):
    norm, hidden, qkv = counts
    shapes = [items[0].shape] + [(norm,)] * 5 + [(hidden,), (qkv,), (norm,)]
    return call(
        total_kernel,
        (1,),
        [whole_spec(item.shape) for item in (*items, *rows)] + kept(wait),
        [whole_spec(shape) for shape in shapes],
        [jax.ShapeDtypeStruct(shape, F32) for shape in shapes],
        [],
        "total",
        prefetch=1,
    )(at, *items, *rows, *wait)


def gate_kernel(*refs):
    pass


def gate(items, wait):
    return call(
        gate_kernel,
        (1,),
        kept((*items, *wait)),
        kept(items),
        [jax.ShapeDtypeStruct(item.shape, item.dtype) for item in items],
        [],
        "gate",
        aliases={index: index for index in range(len(items))},
    )(*items, *wait)


def swap(value, axis, bits):
    count = lax.axis_size(axis)
    return lax.ppermute(value, axis, [(i, i ^ bits) for i in range(count)])


def gather_group(own):
    far = swap(own, "tensor", 2)
    near = swap(own, "tensor", 1)
    return (own, near, far, swap(far, "tensor", 1))


def scatter_group(slabs):
    far = (slabs[2].astype(F32) + swap(slabs[3], "tensor", 1).astype(F32)).astype(BF16)
    return (slabs[0], swap(slabs[1], "tensor", 1), swap(far, "tensor", 2)), (far,)


PARTNERS = (0, 2, 4, 6, 1, 3, 5, 7)


def paired():
    return lax.axis_size("dp") == len(PARTNERS)


def feature_order():
    if paired():
        return jnp.array(PARTNERS, jnp.int32) ^ lax.axis_index("dp").astype(jnp.int32)
    return jnp.zeros((1,), jnp.int32)


def gather_rows(own):
    if not paired():
        return (lax.all_gather(own, "dp", axis=0, tiled=True),)
    same = [own] + [swap(own, "dp", bits) for bits in PARTNERS[1:4]]
    return (*same, *(swap(piece, "dp", 1) for piece in same))


def partner_sums(own, sent):
    kept_block, *outward = halve(own, swap(sent, "dp", 1), ())
    return (kept_block, *(swap(half, "dp", bits) for half, bits in zip(outward, PARTNERS[1:4])))


def vector_sums(norms, others, wait):
    (rows,) = gate([jnp.concatenate([norms, others], axis=0)], wait)
    rows = rows + swap(rows, "dp", 1)
    return (rows, *(swap(rows, "dp", bits) for bits in PARTNERS[1:4]))


def body(
    tokens,
    segment_ids,
    ln1_gain,
    ln1_bias,
    ln2_gain,
    ln2_bias,
    w_qkv,
    b_qkv,
    w_dense,
    b_dense,
    w_fc1,
    b_fc1,
    w_fc2,
    b_fc2,
    cotangent,
):
    group_rows = segment_ids.shape[0]
    width = tokens.shape[1]
    own_width = w_qkv.shape[0]
    dp_count = lax.axis_size("dp")
    tensor_count = lax.axis_size("tensor")
    mine = lax.axis_index("tensor").astype(jnp.int32)
    place = mine.reshape(1)
    order = feature_order()

    firsts = gather_rows(w_qkv)
    x_all = gather_group(turn(order, tokens))
    weights = lax.all_gather(jnp.concatenate([w_fc1, w_fc2, w_dense], axis=1), "dp", axis=0, tiled=True)
    rows = jnp.stack([ln1_gain, ln1_bias, ln2_gain, ln2_bias, b_fc1, jnp.pad(b_qkv, (0, width - b_qkv.shape[0])), b_dense + b_fc2])
    columns = stand(order, jnp.pad(rows, ((0, 1), (0, 0))), ())
    (dy_own,) = gate([turn(order, cotangent)], (x_all[2], *firsts[4:]))
    dy_far, dy_near = swap(dy_own, "tensor", 2), swap(dy_own, "tensor", 1)

    row = jnp.arange(group_rows, dtype=jnp.int32)
    padding = segment_ids != segment_ids[0]
    length = jnp.sum(jnp.where(padding, 0, 1))
    starts = jnp.where(padding, length, 0)
    inverse = 10000.0 ** (-jnp.arange(0, ROT, 2, dtype=F32) / ROT)
    angles = inverse[:, None] * (row - starts).astype(F32)[None, :]
    cosine, sine = jnp.cos(angles), jnp.sin(angles)
    starts = starts[None, :]

    qkv, normed_one, normed_two = project(place, x_all, firsts, columns, cosine, sine, (dy_own,))
    heads = range(qkv.shape[0] // (3 * HEAD))
    attended, lse = [], []
    for head in heads:
        through = (dy_far,) if head == 1 else ()
        result, scale, *through = attend(starts, qkv, head, 1, attended[-1:], through)
        attended.append(result)
        lse.append(scale)
        if head == 1:
            (dy_far,) = through
    dy_all = (dy_own, dy_near, dy_far, swap(dy_far, "tensor", 1))
    *branch, part, att_grad, feed_grads, feed_vectors = feed(
        place, order, dy_all, normed_two, weights, attended, columns
    )
    feed_grads = lax.psum_scatter(feed_grads, "dp", scatter_dimension=0, tiled=True)
    counts = (w_fc1.shape[1], w_fc2.shape[1], w_dense.shape[1])
    out_summands, branch_wait = scatter_group(branch)

    mixed_grad = []
    for head in heads:
        wait = (*branch_wait, *mixed_grad[-1:]) if head == 1 else mixed_grad[-1:]
        mixed_grad.append(
            attend_back(starts, cosine, sine, qkv, att_grad, attended[head], lse[head], head, wait)
        )
    *unit_grad, qkv_own, qkv_sent, last_vectors = project_back(
        place, order, normed_one, firsts, mixed_grad, part, columns, out_summands[2:]
    )
    norms = jnp.concatenate([last_vectors[0:2], feed_vectors[0:2]], axis=0)
    others = jnp.concatenate([feed_vectors[2:4], last_vectors[2:4]], axis=0)
    if paired():
        norms = norms + swap(norms, "tensor", 1) + swap(norms, "tensor", 2) + swap(norms, "tensor", 3)
    else:
        norms = lax.psum(norms, "tensor")
    far = share(unit_grad[2], swap(unit_grad[3], "tensor", 1), (norms,))
    summands = (unit_grad[0], swap(unit_grad[1], "tensor", 1), swap(far, "tensor", 2))
    input_grad = finish(
        finish_grad_kernel, order, summands, x_all[0], dy_own, F32, "finish_grad", 0
    )
    out = finish(
        finish_out_kernel, order, out_summands, x_all[0], columns, BF16, "finish_out", 0, (far,)
    )
    norm_count, bias_count = own_width // tensor_count, b_qkv.shape[0] // dp_count
    at = lax.axis_index("dp").astype(jnp.int32) * jnp.array([own_width, own_width, bias_count], jnp.int32)
    at = at + mine * jnp.array([norm_count, 0, 0], jnp.int32)
    up_grad, down_grad, dense_grad = parts(feed_grads, counts, (input_grad,))
    if paired():
        qkv_grads, *vectors = total(
            at,
            partner_sums(qkv_own, qkv_sent),
            vector_sums(norms, others, (out,)),
            (norm_count, own_width, bias_count),
            (input_grad,),
        )
    else:
        qkv_grads = jnp.concatenate([qkv_own, qkv_sent], axis=0)
        qkv_grads = lax.psum_scatter(qkv_grads, "dp", scatter_dimension=0, tiled=True).astype(F32)
        rows = lax.psum(jnp.concatenate([norms, others], axis=0), "dp")
        vectors = [lax.dynamic_slice_in_dim(rows[index], at[0], norm_count, 0) for index in range(5)]
        vectors += [lax.dynamic_slice_in_dim(rows[5], at[1], own_width, 0)]
        vectors += [lax.dynamic_slice_in_dim(rows[6], at[2], bias_count, 0), vectors[4]]
    return (
        out,
        input_grad,
        *vectors[:4],
        qkv_grads,
        vectors[6],
        dense_grad,
        vectors[4],
        up_grad,
        vectors[5],
        down_grad,
        vectors[7],
    )


def solution(mesh):
    placed = (
        P(("dp", "tensor"), None),
        P("dp"),
        P(),
        P(),
        P(),
        P(),
        P("dp", "tensor"),
        P("tensor"),
        P("dp", "tensor"),
        P(),
        P("dp", "tensor"),
        P("tensor"),
        P("dp", "tensor"),
        P(),
        P(("dp", "tensor"), None),
    )
    return jax.shard_map(
        body,
        mesh=mesh,
        in_specs=placed,
        out_specs=(
            P(("dp", "tensor"), None),
            P(("dp", "tensor"), None),
            P(("dp", "tensor")),
            P(("dp", "tensor")),
            P(("dp", "tensor")),
            P(("dp", "tensor")),
            P("dp", "tensor"),
            P(("tensor", "dp")),
            P("dp", "tensor"),
            P(("dp", "tensor")),
            P("dp", "tensor"),
            P(("tensor", "dp")),
            P("dp", "tensor"),
            P(("dp", "tensor")),
        ),
        check_vma=False,
    )
```
